32 devices in a mesh: groups: 2 (over x), dp: 8 (over z, y), tensor: 2 (over core).
Axes of the slice: x: 2, y: 2, z: 4, core: 2. Of those that a mesh axis runs over, the one named last changes fastest.
Arguments:
- hidden: bfloat16 [12288, 8192], P(('groups', 'dp', 'tensor')), parts along dimension 0, may hold values from -64 to 64
- norm_gain: bfloat16 [8192], replicated, may hold values from 0.099609375 to 1.8984375
- key_weight: bfloat16 [8192, 512], P(None, 'tensor'), may hold values from -0.0625 to 0.0625
- value_weight: bfloat16 [8192, 512], P(None, 'tensor'), may hold values from -0.0625 to 0.0625
- queries: bfloat16 [12288, 4096], P(('groups', 'dp'), 'tensor'), parts along dimension 0, may hold values from -300 to 300
- segment_ids: int32 [12288], P(('groups', 'dp')), parts along dimension 0, may hold values from 0 to 7, as said below
- prompt_lengths: int32 [16, 8], P(('groups', 'dp')), parts along dimension 0, may hold values from 1 to 192, as said below
- prompt_offsets: int32 [16, 8], P(('groups', 'dp')), parts along dimension 0, may hold values from 0 to 767, as said below
- decode_owner: int32 [16, 8], P(('groups', 'dp')), parts along dimension 0, may hold values from 0 to 7, as said below
- slot_offsets: int32 [16, 8], P(('groups', 'dp')), parts along dimension 0, may hold values from 0 to 1535, as said below
Outputs:
- attended: bfloat16 [12288, 4096], P(('groups', 'dp'), 'tensor'), parts along dimension 0
- key_cache: bfloat16 [16, 1536, 512], P(('groups', 'dp'), None, 'tensor'), parts along dimension 0
- value_cache: bfloat16 [16, 1536, 512], P(('groups', 'dp'), None, 'tensor'), parts along dimension 0
The draws below stay inside these ranges and needn't reach their ends.
There are 2 independent parts, one for each index of `groups`. The reference program is written for one: setup_inputs(seed, part) draws one part's arguments, and reference() takes and returns one part's arrays. A program takes and returns all parts, laid end to end along the dimension named above; an argument that names none is the same for every part. Nothing has to cross between parts.
Inputs may be any that keep to these rules, and one draw needn't show every extreme that they name: `prompt_lengths`: the 8 lengths of a pack sum to 768; every pack has a prompt of exactly 192 tokens. `prompt_offsets`: 0 for a pack's first prompt, then the running sum of the lengths before it. `segment_ids`: row t of a pack belongs to prompt s where prompt_offsets[p, s] <= t < prompt_offsets[p, s] + prompt_lengths[p, s]. `decode_owner`: in every pack each owner receives exactly one prompt. `slot_offsets`: the prompt of pack p lies in slots p * 192 to (p + 1) * 192 - 1 of its owner's cache.
All inputs are finite; a program needn't handle non-finite values.
Results may differ from the reference program's by a relative error of at most 0.011.
Values may be sent and summed in bfloat16 or wider, within the bound.
No kernel may reach another device: no remote copies, remote signals or barrier semaphores. Data moves between devices by JAX's collectives and lax.ppermute only.
A program may use at most 192 MiB of HBM per device.

```python
import math
import jax
import jax.numpy as jnp
from jax import lax

D = 8192
HQ = 32
KVH = 4
HD = 128
TOK_ROW = 768
TOKENS = 6144
SEQS = 8
MAXLEN = 192
CACHE = 1536
N_DP = 8


def prompt_layout(key):

    def one_pack(pack_key):
        key_short, key_second, key_order = jax.random.split(pack_key, 3)
        short_part = jax.random.randint(key_short, (SEQS // 2,), 1, MAXLEN, dtype=jnp.int32)
        paired = jnp.stack([short_part, MAXLEN - short_part], axis=1).reshape(-1)
        second_len = jax.random.randint(key_second, (), 1, MAXLEN - 1, dtype=jnp.int32)
        fourth_len = MAXLEN - second_len - 1
        leading = jnp.stack([jnp.int32(MAXLEN) + 0 * second_len, second_len, fourth_len]).astype(jnp.int32)
        ordered = jnp.concatenate([leading, paired[4:]])
        shuffle = jax.random.permutation(key_order, SEQS - 1).astype(jnp.int32)
        lengths = jnp.concatenate([ordered[shuffle], jnp.ones((1,), jnp.int32)]).astype(jnp.int32)
        offsets = (jnp.cumsum(lengths) - lengths).astype(jnp.int32)
        row_index = jnp.arange(TOK_ROW, dtype=jnp.int32)
        segment = jnp.sum((row_index[:, None] >= offsets[None, :]).astype(jnp.int32), axis=1) - 1
        return (lengths, offsets, segment.astype(jnp.int32))
    pack_keys = jax.random.split(key, SEQS)
    return jax.vmap(one_pack)(pack_keys)


def draw_segment_ids(key, part):
    layout = prompt_layout(key)
    return layout[2].reshape(-1)


def draw_prompt_lengths(key, part):
    layout = prompt_layout(key)
    return layout[0]


def draw_prompt_offsets(key, part):
    layout = prompt_layout(key)
    return layout[1]


def draw_decode_owner(key, part):
    key = jax.random.fold_in(key, 19)
    pack_keys = jax.random.split(key, SEQS)

    def one_pack(pack_key):
        return jax.random.permutation(pack_key, SEQS).astype(jnp.int32)
    return jax.vmap(one_pack)(pack_keys)


def draw_slot_offsets(key, part):
    layout = prompt_layout(key)
    key = jax.random.fold_in(key, 23)
    room = MAXLEN - layout[0] + 1
    jitter = jax.random.randint(key, (SEQS, SEQS), 0, 1 << 20, dtype=jnp.int32) % room
    jitter = jitter.at[:, SEQS - 1].set(room[:, SEQS - 1] - 1)
    return (jnp.arange(SEQS, dtype=jnp.int32)[:, None] * MAXLEN + jitter).astype(jnp.int32)


def draw_hidden(key, part):
    key = jax.random.fold_in(key, 29)
    key_rows, key_cols, key_base = jax.random.split(key, 3)
    row_scale = jnp.exp(jax.random.uniform(key_rows, (TOKENS, 1), minval=math.log(0.5), maxval=math.log(5.0)))
    col_scale = jnp.exp(jax.random.uniform(key_cols, (1, D), minval=math.log(0.3), maxval=math.log(3.0)))
    values = jax.random.truncated_normal(key_base, -4.0, 4.0, (TOKENS, D)) * row_scale * col_scale
    return values.astype(jnp.bfloat16)


def draw_queries(key, part):
    key = jax.random.fold_in(key, 31)
    key_base = jax.random.fold_in(key, 0)
    values = jax.random.truncated_normal(key_base, -5.0, 5.0, (TOKENS, HQ * HD))
    return values.astype(jnp.bfloat16)


def level_of(stream_key, extent, cuts, smallest, top_value):
    factor_of = 1.0
    for position, parts in cuts:
        draws = jax.random.uniform(jax.random.fold_in(jax.random.fold_in(stream_key, 6), position), (parts,), jnp.float32, smallest / len(cuts), top_value / len(cuts))
        factor_of = factor_of * jnp.repeat(jnp.exp(draws), extent[position] // parts).reshape((-1,) + (1,) * (len(extent) - 1 - position))
    return factor_of


def scatter_about(key, shape, scale, limit, cuts=(), held_as=jnp.bfloat16):
    gain = level_of(key, shape, cuts, -0.22, 0.18) if cuts else 1.0
    values = jax.random.normal(key, shape, jnp.float32) * scale * gain
    return jnp.minimum(jnp.maximum(values, -limit), limit).astype(held_as)


def setup_inputs(seed: int = 0, part: int = 0) -> dict:
    keys = jax.random.split(jax.random.key(seed), 11)
    part_splits = jax.random.split(jax.random.fold_in(keys[10], part), 11)
    hidden = draw_hidden(jax.random.fold_in(jax.random.fold_in(keys[10], part), 71), part)
    norm_gain = jnp.clip(1.0 + 0.18 * jax.random.normal(keys[1], (D,), jnp.float32), 0.099609375, 1.8984375).astype(jnp.bfloat16)
    key_weight = scatter_about(keys[2], (D, KVH * HD), D ** -0.5, 0.0625, ((1, 2),))
    value_weight = scatter_about(keys[3], (D, KVH * HD), D ** -0.5, 0.0625, ((1, 2),))
    queries = draw_queries(jax.random.fold_in(jax.random.fold_in(keys[10], part), 71), part)
    segment_ids = draw_segment_ids(jax.random.fold_in(jax.random.fold_in(keys[10], part), 71), part)
    prompt_lengths = draw_prompt_lengths(jax.random.fold_in(jax.random.fold_in(keys[10], part), 71), part)
    prompt_offsets = draw_prompt_offsets(jax.random.fold_in(jax.random.fold_in(keys[10], part), 71), part)
    decode_owner = draw_decode_owner(jax.random.fold_in(jax.random.fold_in(keys[10], part), 71), part)
    slot_offsets = draw_slot_offsets(jax.random.fold_in(jax.random.fold_in(keys[10], part), 71), part)
    return dict(hidden=hidden, norm_gain=norm_gain, key_weight=key_weight, value_weight=value_weight, queries=queries, segment_ids=segment_ids, prompt_lengths=prompt_lengths, prompt_offsets=prompt_offsets, decode_owner=decode_owner, slot_offsets=slot_offsets)


epsilon = 1e-05
rope_base = 500000.0

def normalize(row_block, gain_vector):
    floats = row_block.astype(jnp.float32)
    factor = lax.rsqrt(lax.optimization_barrier(jnp.mean(floats * floats, axis=-1, keepdims=True)) + epsilon)
    return (floats * factor * gain_vector.astype(jnp.float32)).astype(jnp.bfloat16)

def rotate(key_floats, positions):
    half_dim = HD // 2
    inverse_freq = rope_base ** (-(jnp.arange(half_dim, dtype=jnp.float32) * 2.0) / HD)
    angles = positions.astype(jnp.float32)[:, None] * inverse_freq[None, :]
    cosine = jnp.cos(angles)[:, None, :]
    sine_part = jnp.sin(angles)[:, None, :]
    shaped = key_floats.reshape(key_floats.shape[0], -1, HD)
    first_half = shaped[..., :half_dim]
    second_half = shaped[..., half_dim:]
    turned = jnp.concatenate([first_half * cosine - second_half * sine_part, second_half * cosine + first_half * sine_part], axis=-1)
    return turned.reshape(key_floats.shape)

def attend_pack(packed_block):
    query_block, key_block, value_block, segment_block = packed_block
    group_size = HQ // KVH
    query_four = query_block.reshape(TOK_ROW, KVH, group_size, HD).astype(jnp.float32)
    key_three = key_block.reshape(TOK_ROW, KVH, HD).astype(jnp.float32)
    value_three = value_block.reshape(TOK_ROW, KVH, HD).astype(jnp.float32)
    scores = jnp.einsum('qgrd,kgd->grqk', query_four, key_three) * HD ** (-0.5)
    row_index = jnp.arange(TOK_ROW, dtype=jnp.int32)
    allowed = (segment_block[:, None] == segment_block[None, :]) & (row_index[None, :] <= row_index[:, None])
    scores = jnp.where(allowed, scores, -1e+30)
    maxima = lax.optimization_barrier(jnp.max(scores, axis=-1, keepdims=True))
    exponent = jnp.exp(scores - maxima)
    totals = lax.optimization_barrier(jnp.sum(exponent, axis=-1, keepdims=True))
    weights = (exponent / totals).astype(jnp.bfloat16)
    output = jnp.einsum('grqk,kgd->qgrd', weights.astype(jnp.float32), value_three)
    return output.reshape(TOK_ROW, HQ * HD).astype(jnp.bfloat16)

def reference(hidden, norm_gain, key_weight, value_weight, queries, segment_ids, prompt_lengths, prompt_offsets, decode_owner, slot_offsets):
    normed = normalize(hidden, norm_gain)
    key_floats = jnp.dot(normed, key_weight, preferred_element_type=jnp.float32)
    value_floats = jnp.dot(normed, value_weight, preferred_element_type=jnp.float32)
    row_index = jnp.arange(TOKENS, dtype=jnp.int32)
    pack_index = row_index // TOK_ROW
    within = row_index % TOK_ROW - prompt_offsets[pack_index, segment_ids]
    key_rows = rotate(key_floats, within).astype(jnp.bfloat16)
    value_rows = value_floats.astype(jnp.bfloat16)
    blocks = (queries.reshape(N_DP, TOK_ROW, HQ * HD), key_rows.reshape(N_DP, TOK_ROW, KVH * HD), value_rows.reshape(N_DP, TOK_ROW, KVH * HD), segment_ids.reshape(N_DP, TOK_ROW))
    attended = lax.map(attend_pack, blocks).reshape(TOKENS, HQ * HD)
    owner_row = decode_owner[pack_index, segment_ids]
    length_row = prompt_lengths[pack_index, segment_ids]
    owner_row = jnp.where(within < length_row, owner_row, N_DP)
    slot_row = slot_offsets[pack_index, segment_ids] + within
    empty_cache = jnp.zeros((N_DP, CACHE, KVH * HD), jnp.bfloat16)
    key_cache = empty_cache.at[owner_row, slot_row].set(key_rows, mode='drop')
    value_cache = empty_cache.at[owner_row, slot_row].set(value_rows, mode='drop')
    return (attended, key_cache, value_cache)
```

```python
import functools

import jax
import jax.numpy as jnp
import numpy as np
from jax import lax
from jax.experimental import pallas as pl
from jax.experimental.pallas import tpu as pltpu
from jax.sharding import PartitionSpec as P

HD = 128
EPSILON = 1e-05
ROPE_BASE = 500000.0
MIB = 1024 * 1024
SMEM = pl.BlockSpec(memory_space=pltpu.SMEM)
VMEM = pl.BlockSpec(memory_space=pltpu.VMEM)


def prompt_start(rows, offset_ref):
    start = jnp.zeros_like(rows)
    for s in range(offset_ref.shape[1]):
        offset = offset_ref[0, s]
        start = jnp.where(rows >= offset, jnp.maximum(start, offset), start)
    return start


def rotation_tables(block, offset_ref, cos_ref, sin_ref):
    position = lax.broadcasted_iota(jnp.int32, (block, HD), 0).astype(jnp.float32)
    lane = lax.broadcasted_iota(jnp.int32, (block, HD), 1)
    half = lax.broadcasted_iota(jnp.int32, (1, HD), 1) % (HD // 2)
    inverse = jnp.zeros((1, HD), jnp.float32)
    for i in range(HD // 2):
        inverse = jnp.where(half == i, np.float32(ROPE_BASE ** (-2.0 * i / HD)), inverse)
    angle = position * inverse
    cosine = jnp.cos(angle)
    sine = jnp.where(lane < HD // 2, -1.0, 1.0) * jnp.sin(angle)
    for s in range(offset_ref.shape[1]):
        rows = pl.ds(offset_ref[0, s], block)
        cos_ref[rows, :] = cosine
        sin_ref[rows, :] = sine


def project(h_ref, gain_ref, wk_ref, wv_ref, acc_k, acc_v, squares, chunk, ready=None):
    for c in range(h_ref.shape[1] // chunk):
        if ready is not None:
            ready(c)
        at = slice(c * chunk, (c + 1) * chunk)
        h = h_ref[:, at]
        scaled = h * gain_ref[:, at]
        key = jnp.dot(scaled, wk_ref[at, :], preferred_element_type=jnp.float32)
        value = jnp.dot(scaled, wv_ref[at, :], preferred_element_type=jnp.float32)
        parts = [h[:, j * HD : (j + 1) * HD].astype(jnp.float32) for j in range(chunk // HD)]
        total = sum(p * p for p in parts)
        if c == 0:
            acc_k[...], acc_v[...], squares[...] = key, value, total
        else:
            acc_k[...] += key
            acc_v[...] += value
            squares[...] += total


def finish(width, cosine, sine, acc_k, acc_v, squares):
    factor = lax.rsqrt(jnp.sum(squares[...], axis=1, keepdims=True) / width + EPSILON)
    keys = []
    for h in range(acc_k.shape[1] // HD):
        x = acc_k[:, h * HD : (h + 1) * HD] * factor
        keys.append((x * cosine + pltpu.roll(x, HD // 2, 1) * sine).astype(jnp.bfloat16))
    return jnp.concatenate(keys, axis=1), (acc_v[...] * factor).astype(jnp.bfloat16)


def own_kernel(
    block, chunk, offset_ref, h_hbm, wk_hbm, wv_hbm, gain_ref,
    out_ref, cos_ref, sin_ref, wk_ref, wv_ref, h_ref, acc_k, acc_v, squares, cos_pad, sin_pad, sems
):
    rows, width = h_hbm.shape
    cols = acc_k.shape[1]

    def copies(c):
        at = pl.ds(c * chunk, chunk)
        return (
            pltpu.make_async_copy(h_hbm.at[:, at], h_ref.at[:, at], sems.at[c, 0]),
            pltpu.make_async_copy(wk_hbm.at[at, :], wk_ref.at[at, :], sems.at[c, 1]),
            pltpu.make_async_copy(wv_hbm.at[at, :], wv_ref.at[at, :], sems.at[c, 2]),
        )

    def ready(c):
        for copy in copies(c):
            copy.wait()

    for c in range(width // chunk):
        for copy in copies(c):
            copy.start()
    rotation_tables(block, offset_ref, cos_pad, sin_pad)
    cos_ref[...] = cos_pad[: cos_ref.shape[0], :]
    sin_ref[...] = sin_pad[: sin_ref.shape[0], :]
    project(h_ref, gain_ref, wk_ref, wv_ref, acc_k, acc_v, squares, chunk, ready)
    here = pl.ds(pl.multiple_of(lax.axis_index("tensor") * rows, rows), rows)
    keys, values = finish(width, cos_pad[here, :], sin_pad[here, :], acc_k, acc_v, squares)
    out_ref[:, :cols] = keys
    out_ref[:, cols:] = values


def own_rows(block, offsets, hidden, wk, wv, gain, tok_rows, chunk=1024):
    rows, width = hidden.shape
    cols = wk.shape[1]
    hbm = pl.BlockSpec(memory_space=pltpu.HBM)
    f32 = jnp.float32
    return pl.pallas_call(
        functools.partial(own_kernel, block, chunk),
        in_specs=[SMEM, hbm, hbm, hbm, VMEM],
        out_specs=[VMEM] * 5,
        out_shape=[
            jax.ShapeDtypeStruct((rows, 2 * cols), jnp.bfloat16),
            jax.ShapeDtypeStruct((tok_rows, HD), f32),
            jax.ShapeDtypeStruct((tok_rows, HD), f32),
            jax.ShapeDtypeStruct(wk.shape, wk.dtype),
            jax.ShapeDtypeStruct(wv.shape, wv.dtype),
        ],
        scratch_shapes=[
            pltpu.VMEM((rows, width), jnp.bfloat16),
            pltpu.VMEM((rows, cols), f32),
            pltpu.VMEM((rows, cols), f32),
            pltpu.VMEM((rows, HD), f32),
            pltpu.VMEM((tok_rows + block, HD), f32),
            pltpu.VMEM((tok_rows + block, HD), f32),
            pltpu.SemaphoreType.DMA((width // chunk, 3)),
        ],
        compiler_params=pltpu.CompilerParams(vmem_limit_bytes=44 * MIB),
        cost_estimate=pl.CostEstimate(
            flops=4 * rows * width * cols, bytes_accessed=2 * (rows * width + 2 * width * cols), transcendentals=0
        ),
        name="own_rows",
    )(offsets, hidden, wk, wv, gain)


def select_block(block, cols, owner, places, kv_ref, out_ref):
    offset_ref, length_ref, owner_ref, slot_ref = places
    offset = jnp.int32(0)
    length = jnp.int32(0)
    slot = jnp.int32(0)
    for s in range(owner_ref.shape[1]):
        hit = owner_ref[0, s] == owner
        offset = jnp.where(hit, offset_ref[0, s], offset)
        length = jnp.where(hit, length_ref[0, s], length)
        slot = jnp.where(hit, slot_ref[0, s], slot)
    span = block + 16
    start = jnp.minimum((offset // 16) * 16, kv_ref.shape[0] - span)
    start = pl.multiple_of(start, 16)
    place = lax.broadcasted_iota(jnp.int32, (block, span), 0) + (lax.axis_index("dp") * block - slot)
    token = lax.broadcasted_iota(jnp.int32, (block, span), 1) + (start - offset)
    chosen = (place == token) & (place >= 0) & (place < length)
    picked = jnp.dot(
        jnp.where(chosen, 1.0, 0.0).astype(jnp.bfloat16),
        kv_ref[pl.ds(start, span), :],
        preferred_element_type=jnp.float32,
    ).astype(jnp.bfloat16)
    out_ref[0] = picked[:, :cols]
    out_ref[1] = picked[:, cols:]


def peer_kernel(
    far, block, chunk, offset_ref, length_ref, owner_ref, slot_ref,
    h_ref, wk_ref, wv_ref, gain_ref, cos_ref, sin_ref, own_ref, kv_ref, *rest
):
    blocks, (acc_k, acc_v, squares) = rest[: len(far)], rest[len(far) :]
    rows, width = h_ref.shape
    cols = acc_k.shape[1]
    mine = lax.axis_index("tensor")
    there = pl.ds(pl.multiple_of((1 - mine) * rows, rows), rows)
    here = pl.ds(pl.multiple_of(mine * rows, rows), rows)
    project(h_ref, gain_ref, wk_ref, wv_ref, acc_k, acc_v, squares, chunk)
    keys, values = finish(width, cos_ref[there, :], sin_ref[there, :], acc_k, acc_v, squares)
    kv_ref[there, :cols] = keys
    kv_ref[there, cols:] = values
    kv_ref[here, :] = own_ref[...]
    places = (offset_ref, length_ref, owner_ref, slot_ref)
    for k, out_ref in zip(far, blocks):
        select_block(block, cols, jnp.bitwise_xor(lax.axis_index("dp"), k), places, kv_ref, out_ref)


def peer_rows(far, block, places, peer, wk, wv, gain, cosine, sine, own, chunk=1024):
    rows, width = peer.shape
    cols = wk.shape[1]
    tok_rows = cosine.shape[0]
    return pl.pallas_call(
        functools.partial(peer_kernel, far, block, chunk),
        in_specs=[SMEM] * 4 + [VMEM] * 7,
        out_specs=[VMEM] * (1 + len(far)),
        out_shape=[jax.ShapeDtypeStruct((tok_rows, 2 * cols), jnp.bfloat16)]
        + [jax.ShapeDtypeStruct((2, block, cols), jnp.bfloat16)] * len(far),
        scratch_shapes=[
            pltpu.VMEM((rows, cols), jnp.float32),
            pltpu.VMEM((rows, cols), jnp.float32),
            pltpu.VMEM((rows, HD), jnp.float32),
        ],
        compiler_params=pltpu.CompilerParams(vmem_limit_bytes=28 * MIB),
        cost_estimate=pl.CostEstimate(
            flops=4 * rows * width * cols, bytes_accessed=2 * (rows * width + 2 * width * cols), transcendentals=0
        ),
        name="peer_rows",
    )(*places, peer, wk, wv, gain, cosine, sine, own)


def attend_kernel(tile, window, skipped, near, block, *refs):
    places, (q_ref, kv_ref), rest = refs[:4], refs[4:6], refs[6:]
    if skipped:
        rest = rest[1:]
    out_ref, blocks = rest[0], rest[1:]
    step = pl.program_id(0)
    cols = kv_ref.shape[1] // 2
    groups = cols // HD
    heads = q_ref.shape[1] // HD // groups

    if near:
        @pl.when(step == 0)
        def _():
            for k, block_ref in zip(near, blocks):
                select_block(block, cols, jnp.bitwise_xor(lax.axis_index("dp"), k), places, kv_ref, block_ref)

    first = (step + skipped) * tile
    start = pl.multiple_of(jnp.maximum(first + tile - window, 0), 16)
    row = first + lax.broadcasted_iota(jnp.int32, (tile, window), 0)
    key = start + lax.broadcasted_iota(jnp.int32, (tile, window), 1)
    allowed = (key <= row) & (key >= prompt_start(row, places[0]))
    bias = jnp.where(allowed, 0.0, -1e30)[None]
    ones = jnp.ones((window, HD), jnp.bfloat16)
    scale = HD**-0.5 * float(np.log2(np.e))
    for g in range(groups):
        at = [slice((g * heads + h) * HD, (g * heads + h + 1) * HD) for h in range(heads)]
        q = jnp.concatenate([q_ref[:, a] for a in at], axis=0)
        k = kv_ref[pl.ds(start, window), g * HD : (g + 1) * HD]
        v = kv_ref[pl.ds(start, window), cols + g * HD : cols + (g + 1) * HD]
        scores = lax.dot_general(q, k, (((1,), (1,)), ((), ())), preferred_element_type=jnp.float32)
        scores = scores.reshape(heads, tile, window) * scale + bias
        exponent = jnp.exp2(scores - jnp.max(scores, axis=2, keepdims=True))
        exponent = exponent.astype(jnp.bfloat16).reshape(heads * tile, window)
        summed = jnp.dot(exponent, jnp.concatenate([v, ones], axis=1), preferred_element_type=jnp.float32)
        result = (summed[:, :HD] / summed[:, HD:]).astype(jnp.bfloat16)
        for h, a in enumerate(at):
            out_ref[:, a] = result[h * tile : (h + 1) * tile]


def attend(places, queries, kv, longest, near=(), before=None, tile=64):
    rows, width = queries.shape
    window = tile + longest
    steps = rows // tile // 2
    skipped = 0 if before is None else steps
    cols = kv.shape[1] // 2
    rows_at = pl.BlockSpec((tile, width), lambda i: (i + skipped, 0))
    return pl.pallas_call(
        functools.partial(attend_kernel, tile, window, skipped, near, longest),
        grid=(steps,),
        in_specs=[SMEM] * 4
        + [rows_at, pl.BlockSpec(kv.shape, lambda i: (0, 0))]
        + ([pl.BlockSpec(memory_space=pl.ANY)] if skipped else []),
        out_specs=[rows_at] + [pl.BlockSpec((2, longest, cols), lambda i: (0, 0, 0))] * len(near),
        out_shape=[jax.ShapeDtypeStruct((rows, width), jnp.bfloat16)]
        + [jax.ShapeDtypeStruct((2, longest, cols), jnp.bfloat16)] * len(near),
        input_output_aliases={6: 0} if skipped else {},
        compiler_params=pltpu.CompilerParams(vmem_limit_bytes=32 * MIB),
        cost_estimate=pl.CostEstimate(
            flops=2 * rows * width * window,
            bytes_accessed=2 * rows * width,
            transcendentals=rows * window * width // HD // 2,
        ),
        name="attend_rest" if skipped else "attend_first",
    )(*places, queries, kv, *([before] if skipped else []))


def gather_kernel(n_dp, block, *refs):
    blocks, (key_ref, value_ref, sems) = refs[:n_dp], refs[n_dp:]
    me = lax.axis_index("dp")
    copies = []
    for k in range(n_dp):
        rows = pl.ds(pl.multiple_of(jnp.bitwise_xor(me, k) * block, block), block)
        for n, out_ref in enumerate((key_ref, value_ref)):
            copies.append(pltpu.make_async_copy(blocks[k].at[n], out_ref.at[rows, :], sems.at[k, n]))
    for copy in copies:
        copy.start()
    for copy in copies:
        copy.wait()


def on_device(
    hidden, norm_gain, key_weight, value_weight, queries,
    segment_ids, prompt_lengths, prompt_offsets, decode_owner, slot_offsets,
):
    n_dp = lax.axis_size("dp")
    half, width = hidden.shape
    tok_rows = queries.shape[0]
    cols = key_weight.shape[1]
    block = 2 * tok_rows // n_dp
    gain = norm_gain.reshape(1, width)

    peer = lax.ppermute(hidden, "tensor", [(0, 1), (1, 0)])
    own, cosine, sine, wk, wv = own_rows(
        block, prompt_offsets, hidden, key_weight, value_weight, gain, tok_rows
    )
    places = [prompt_offsets, prompt_lengths, decode_owner, slot_offsets]
    far = tuple(range(n_dp // 2, n_dp))
    near = tuple(range(n_dp // 2))
    swap = lambda a, k: a if k == 0 else lax.ppermute(a, "dp", [(p, p ^ k) for p in range(n_dp)])
    kv, *blocks = peer_rows(far, block, places, peer, wk, wv, gain, cosine, sine, own)
    received = {k: swap(a, k) for k, a in zip(far, blocks)}
    attended, *blocks = attend(places, queries, kv, block, near)
    received.update({k: swap(a, k) for k, a in zip(near, blocks)})
    attended = attend(places, queries, kv, block, (), attended)[0]
    cache = jax.ShapeDtypeStruct((n_dp * block, cols), jnp.bfloat16)
    anywhere = pl.BlockSpec(memory_space=pl.ANY)
    key_cache, value_cache = pl.pallas_call(
        functools.partial(gather_kernel, n_dp, block),
        in_specs=[VMEM] * n_dp,
        out_specs=[anywhere] * 2,
        out_shape=[cache, cache],
        scratch_shapes=[pltpu.SemaphoreType.DMA((n_dp, 2))],
        compiler_params=pltpu.CompilerParams(vmem_limit_bytes=8 * MIB),
        name="place_blocks",
    )(*[received[k] for k in range(n_dp)])
    return attended, key_cache[None], value_cache[None]


def solution(mesh):
    rows = P(("groups", "dp"))
    in_specs = (
        P(("groups", "dp", "tensor"), None),
        P(),
        P(None, "tensor"),
        P(None, "tensor"),
        P(("groups", "dp"), "tensor"),
        rows, rows, rows, rows, rows,
    )
    out_specs = (
        P(("groups", "dp"), "tensor"),
        P(("groups", "dp"), None, "tensor"),
        P(("groups", "dp"), None, "tensor"),
    )
    return jax.shard_map(on_device, mesh=mesh, in_specs=in_specs, out_specs=out_specs, check_vma=False)
```

```python
import functools

import jax
import jax.numpy as jnp
import numpy as np
from jax import lax
from jax.experimental import pallas as pl
from jax.experimental.pallas import tpu as pltpu
from jax.sharding import PartitionSpec as P

HD = 128
EPSILON = 1e-05
ROPE_BASE = 500000.0
MIB = 1024 * 1024
SMEM = pl.BlockSpec(memory_space=pltpu.SMEM)
VMEM = pl.BlockSpec(memory_space=pltpu.VMEM)


def prompt_start(rows, offset_ref):
    start = jnp.zeros_like(rows)
    for s in range(offset_ref.shape[1]):
        offset = offset_ref[0, s]
        start = jnp.where(rows >= offset, jnp.maximum(start, offset), start)
    return start


def rotation_tables(block, offset_ref, cos_ref, sin_ref):
    position = lax.broadcasted_iota(jnp.int32, (block, HD), 0).astype(jnp.float32)
    lane = lax.broadcasted_iota(jnp.int32, (block, HD), 1)
    half = lax.broadcasted_iota(jnp.int32, (1, HD), 1) % (HD // 2)
    inverse = jnp.zeros((1, HD), jnp.float32)
    for i in range(HD // 2):
        inverse = jnp.where(half == i, np.float32(ROPE_BASE ** (-2.0 * i / HD)), inverse)
    angle = position * inverse
    cosine = jnp.cos(angle)
    sine = jnp.where(lane < HD // 2, -1.0, 1.0) * jnp.sin(angle)
    for s in range(offset_ref.shape[1]):
        rows = pl.ds(offset_ref[0, s], block)
        cos_ref[rows, :] = cosine
        sin_ref[rows, :] = sine


def project(h_ref, rows, gain_ref, wk_ref, wv_ref, acc_k, acc_v, squares, chunk, ready=None):
    for c in range(h_ref.shape[1] // chunk):
        if ready is not None:
            ready(c)
        at = slice(c * chunk, (c + 1) * chunk)
        h = h_ref[rows, at]
        scaled = h * gain_ref[:, at]
        key = jnp.dot(scaled, wk_ref[at, :], preferred_element_type=jnp.float32)
        value = jnp.dot(scaled, wv_ref[at, :], preferred_element_type=jnp.float32)
        parts = [h[:, j * HD : (j + 1) * HD].astype(jnp.float32) for j in range(chunk // HD)]
        total = sum(p * p for p in parts)
        if c == 0:
            acc_k[...], acc_v[...], squares[...] = key, value, total
        else:
            acc_k[...] += key
            acc_v[...] += value
            squares[...] += total


def finish(width, cosine, sine, acc_k, acc_v, squares):
    factor = lax.rsqrt(jnp.sum(squares[...], axis=1, keepdims=True) / width + EPSILON)
    keys = []
    for h in range(acc_k.shape[1] // HD):
        x = acc_k[:, h * HD : (h + 1) * HD] * factor
        keys.append((x * cosine + pltpu.roll(x, HD // 2, 1) * sine).astype(jnp.bfloat16))
    return jnp.concatenate(keys, axis=1), (acc_v[...] * factor).astype(jnp.bfloat16)


def own_kernel(
    block, chunk, offset_ref, h_hbm, wk_hbm, wv_hbm, gain_ref,
    out_ref, cos_ref, sin_ref, wk_ref, wv_ref, h_ref, acc_k, acc_v, squares, cos_pad, sin_pad, sems
):
    rows, width = h_hbm.shape
    cols = acc_k.shape[1]

    def copies(c):
        at = pl.ds(c * chunk, chunk)
        return (
            pltpu.make_async_copy(h_hbm.at[:, at], h_ref.at[:, at], sems.at[c, 0]),
            pltpu.make_async_copy(wk_hbm.at[at, :], wk_ref.at[at, :], sems.at[c, 1]),
            pltpu.make_async_copy(wv_hbm.at[at, :], wv_ref.at[at, :], sems.at[c, 2]),
        )

    def ready(c):
        for copy in copies(c):
            copy.wait()

    for c in range(width // chunk):
        for copy in copies(c):
            copy.start()
    rotation_tables(block, offset_ref, cos_pad, sin_pad)
    cos_ref[...] = cos_pad[: cos_ref.shape[0], :]
    sin_ref[...] = sin_pad[: sin_ref.shape[0], :]
    project(h_ref, slice(None), gain_ref, wk_ref, wv_ref, acc_k, acc_v, squares, chunk, ready)
    here = pl.ds(pl.multiple_of(lax.axis_index("tensor") * rows, rows), rows)
    keys, values = finish(width, cos_pad[here, :], sin_pad[here, :], acc_k, acc_v, squares)
    out_ref[:, :cols] = keys
    out_ref[:, cols:] = values


def own_rows(block, offsets, hidden, wk, wv, gain, tok_rows, chunk=1024):
    rows, width = hidden.shape
    cols = wk.shape[1]
    hbm = pl.BlockSpec(memory_space=pltpu.HBM)
    f32 = jnp.float32
    return pl.pallas_call(
        functools.partial(own_kernel, block, chunk),
        in_specs=[SMEM, hbm, hbm, hbm, VMEM],
        out_specs=[VMEM] * 5,
        out_shape=[
            jax.ShapeDtypeStruct((rows, 2 * cols), jnp.bfloat16),
            jax.ShapeDtypeStruct((tok_rows, HD), f32),
            jax.ShapeDtypeStruct((tok_rows, HD), f32),
            jax.ShapeDtypeStruct(wk.shape, wk.dtype),
            jax.ShapeDtypeStruct(wv.shape, wv.dtype),
        ],
        scratch_shapes=[
            pltpu.VMEM((rows, width), jnp.bfloat16),
            pltpu.VMEM((rows, cols), f32),
            pltpu.VMEM((rows, cols), f32),
            pltpu.VMEM((rows, HD), f32),
            pltpu.VMEM((tok_rows + block, HD), f32),
            pltpu.VMEM((tok_rows + block, HD), f32),
            pltpu.SemaphoreType.DMA((width // chunk, 3)),
        ],
        compiler_params=pltpu.CompilerParams(vmem_limit_bytes=44 * MIB),
        cost_estimate=pl.CostEstimate(
            flops=4 * rows * width * cols, bytes_accessed=2 * (rows * width + 2 * width * cols), transcendentals=0
        ),
        name="own_rows",
    )(offsets, hidden, wk, wv, gain)


def select_block(block, cols, owner, places, kv_ref, out_ref):
    offset_ref, length_ref, owner_ref, slot_ref = places
    offset = jnp.int32(0)
    length = jnp.int32(0)
    slot = jnp.int32(0)
    for s in range(owner_ref.shape[1]):
        hit = owner_ref[0, s] == owner
        offset = jnp.where(hit, offset_ref[0, s], offset)
        length = jnp.where(hit, length_ref[0, s], length)
        slot = jnp.where(hit, slot_ref[0, s], slot)
    span = block + 16
    start = jnp.minimum((offset // 16) * 16, kv_ref.shape[0] - span)
    start = pl.multiple_of(start, 16)
    place = lax.broadcasted_iota(jnp.int32, (block, span), 0) + (lax.axis_index("dp") * block - slot)
    token = lax.broadcasted_iota(jnp.int32, (block, span), 1) + (start - offset)
    chosen = (place == token) & (place >= 0) & (place < length)
    picked = jnp.dot(
        jnp.where(chosen, 1.0, 0.0).astype(jnp.bfloat16),
        kv_ref[pl.ds(start, span), :],
        preferred_element_type=jnp.float32,
    ).astype(jnp.bfloat16)
    out_ref[0] = picked[:, :cols]
    out_ref[1] = picked[:, cols:]


def first_kernel(
    owner, block, chunk, offset_ref, length_ref, owner_ref, slot_ref,
    h_ref, wk_ref, wv_ref, gain_ref, cos_ref, sin_ref, own_ref, block_ref, kv, acc_k, acc_v, squares
):
    rows, width = h_ref.shape
    cols = acc_k.shape[1]
    span = acc_k.shape[0]
    mine = lax.axis_index("tensor")
    owner = jnp.bitwise_xor(lax.axis_index("dp"), owner)
    here = pl.ds(pl.multiple_of(mine * rows, rows), rows)
    kv[here, :] = own_ref[...]
    offset = jnp.int32(0)
    for s in range(owner_ref.shape[1]):
        offset = jnp.where(owner_ref[0, s] == owner, offset_ref[0, s], offset)
    start = jnp.minimum((offset // 16) * 16, 2 * rows - span)
    local = pl.multiple_of(jnp.clip(start - (1 - mine) * rows, 0, rows - span), 16)
    there = pl.ds(pl.multiple_of((1 - mine) * rows + local, 16), span)
    project(h_ref, pl.ds(local, span), gain_ref, wk_ref, wv_ref, acc_k, acc_v, squares, chunk)
    keys, values = finish(width, cos_ref[there, :], sin_ref[there, :], acc_k, acc_v, squares)
    kv[there, :cols] = keys
    kv[there, cols:] = values
    select_block(block, cols, owner, (offset_ref, length_ref, owner_ref, slot_ref), kv, block_ref)


def first_block(owner, block, places, peer, wk, wv, gain, cosine, sine, own, chunk=1024):
    rows, width = peer.shape
    cols = wk.shape[1]
    span = block + 16
    return pl.pallas_call(
        functools.partial(first_kernel, owner, block, chunk),
        in_specs=[SMEM] * 4 + [VMEM] * 7,
        out_specs=VMEM,
        out_shape=jax.ShapeDtypeStruct((2, block, cols), jnp.bfloat16),
        scratch_shapes=[
            pltpu.VMEM((2 * rows, 2 * cols), jnp.bfloat16),
            pltpu.VMEM((span, cols), jnp.float32),
            pltpu.VMEM((span, cols), jnp.float32),
            pltpu.VMEM((span, HD), jnp.float32),
        ],
        compiler_params=pltpu.CompilerParams(vmem_limit_bytes=28 * MIB),
        cost_estimate=pl.CostEstimate(
            flops=4 * span * width * cols, bytes_accessed=2 * (span * width + 2 * width * cols), transcendentals=0
        ),
        name="first_block",
    )(*places, peer, wk, wv, gain, cosine, sine, own)


def peer_kernel(
    far, block, chunk, offset_ref, length_ref, owner_ref, slot_ref,
    h_ref, wk_ref, wv_ref, gain_ref, cos_ref, sin_ref, own_ref, kv_ref, *rest
):
    blocks, (acc_k, acc_v, squares) = rest[: len(far)], rest[len(far) :]
    rows, width = h_ref.shape
    cols = acc_k.shape[1]
    mine = lax.axis_index("tensor")
    there = pl.ds(pl.multiple_of((1 - mine) * rows, rows), rows)
    here = pl.ds(pl.multiple_of(mine * rows, rows), rows)
    project(h_ref, slice(None), gain_ref, wk_ref, wv_ref, acc_k, acc_v, squares, chunk)
    keys, values = finish(width, cos_ref[there, :], sin_ref[there, :], acc_k, acc_v, squares)
    kv_ref[there, :cols] = keys
    kv_ref[there, cols:] = values
    kv_ref[here, :] = own_ref[...]
    places = (offset_ref, length_ref, owner_ref, slot_ref)
    for k, out_ref in zip(far, blocks):
        select_block(block, cols, jnp.bitwise_xor(lax.axis_index("dp"), k), places, kv_ref, out_ref)


def peer_rows(far, block, places, peer, wk, wv, gain, cosine, sine, own, chunk=1024):
    rows, width = peer.shape
    cols = wk.shape[1]
    tok_rows = cosine.shape[0]
    return pl.pallas_call(
        functools.partial(peer_kernel, far, block, chunk),
        in_specs=[SMEM] * 4 + [VMEM] * 7,
        out_specs=[VMEM] * (1 + len(far)),
        out_shape=[jax.ShapeDtypeStruct((tok_rows, 2 * cols), jnp.bfloat16)]
        + [jax.ShapeDtypeStruct((2, block, cols), jnp.bfloat16)] * len(far),
        scratch_shapes=[
            pltpu.VMEM((rows, cols), jnp.float32),
            pltpu.VMEM((rows, cols), jnp.float32),
            pltpu.VMEM((rows, HD), jnp.float32),
        ],
        compiler_params=pltpu.CompilerParams(vmem_limit_bytes=28 * MIB),
        cost_estimate=pl.CostEstimate(
            flops=4 * rows * width * cols, bytes_accessed=2 * (rows * width + 2 * width * cols), transcendentals=0
        ),
        name="peer_rows",
    )(*places, peer, wk, wv, gain, cosine, sine, own)


def attend_kernel(tile, window, offset_ref, q_ref, kv_ref, out_ref):
    cols = kv_ref.shape[1] // 2
    groups = cols // HD
    heads = q_ref.shape[1] // HD // groups
    first = pl.program_id(0) * tile
    start = pl.multiple_of(jnp.maximum(first + tile - window, 0), 16)
    row = first + lax.broadcasted_iota(jnp.int32, (tile, window), 0)
    key = start + lax.broadcasted_iota(jnp.int32, (tile, window), 1)
    allowed = (key <= row) & (key >= prompt_start(row, offset_ref))
    bias = jnp.where(allowed, 0.0, -1e30)[None]
    ones = jnp.ones((window, HD), jnp.bfloat16)
    scale = HD**-0.5 * float(np.log2(np.e))
    for g in range(groups):
        at = [slice((g * heads + h) * HD, (g * heads + h + 1) * HD) for h in range(heads)]
        q = jnp.concatenate([q_ref[:, a] for a in at], axis=0)
        k = kv_ref[pl.ds(start, window), g * HD : (g + 1) * HD]
        v = kv_ref[pl.ds(start, window), cols + g * HD : cols + (g + 1) * HD]
        scores = lax.dot_general(q, k, (((1,), (1,)), ((), ())), preferred_element_type=jnp.float32)
        scores = scores.reshape(heads, tile, window) * scale + bias
        exponent = jnp.exp2(scores - jnp.max(scores, axis=2, keepdims=True))
        exponent = exponent.astype(jnp.bfloat16).reshape(heads * tile, window)
        summed = jnp.dot(exponent, jnp.concatenate([v, ones], axis=1), preferred_element_type=jnp.float32)
        result = (summed[:, :HD] / summed[:, HD:]).astype(jnp.bfloat16)
        for h, a in enumerate(at):
            out_ref[:, a] = result[h * tile : (h + 1) * tile]


def attend(offsets, queries, kv, longest, tile=64):
    rows, width = queries.shape
    window = tile + longest
    rows_at = pl.BlockSpec((tile, width), lambda i: (i, 0))
    return pl.pallas_call(
        functools.partial(attend_kernel, tile, window),
        grid=(rows // tile,),
        in_specs=[SMEM, rows_at, pl.BlockSpec(kv.shape, lambda i: (0, 0))],
        out_specs=rows_at,
        out_shape=jax.ShapeDtypeStruct((rows, width), jnp.bfloat16),
        compiler_params=pltpu.CompilerParams(vmem_limit_bytes=32 * MIB),
        cost_estimate=pl.CostEstimate(
            flops=4 * rows * width * window,
            bytes_accessed=4 * rows * width,
            transcendentals=rows * window * width // HD,
        ),
        name="attend",
    )(offsets, queries, kv)


def gather_kernel(order, block, *refs):
    blocks, (key_ref, value_ref, sems) = refs[: len(order)], refs[len(order) :]
    me = lax.axis_index("dp")
    copies = []
    for i, k in enumerate(order):
        rows = pl.ds(pl.multiple_of(jnp.bitwise_xor(me, k) * block, block), block)
        for n, out_ref in enumerate((key_ref, value_ref)):
            copies.append(pltpu.make_async_copy(blocks[i].at[n], out_ref.at[rows, :], sems.at[i, n]))
    for copy in copies:
        copy.start()
    for copy in copies:
        copy.wait()


def on_device(
    hidden, norm_gain, key_weight, value_weight, queries,
    segment_ids, prompt_lengths, prompt_offsets, decode_owner, slot_offsets,
):
    n_dp = lax.axis_size("dp")
    half, width = hidden.shape
    tok_rows = queries.shape[0]
    cols = key_weight.shape[1]
    block = 2 * tok_rows // n_dp
    gain = norm_gain.reshape(1, width)

    peer = lax.ppermute(hidden, "tensor", [(0, 1), (1, 0)])
    own, cosine, sine, wk, wv = own_rows(
        block, prompt_offsets, hidden, key_weight, value_weight, gain, tok_rows
    )
    places = [prompt_offsets, prompt_lengths, decode_owner, slot_offsets]
    swap = lambda a, k: lax.ppermute(a, "dp", [(p, p ^ k) for p in range(n_dp)]) if k else a
    half_dp = n_dp // 2
    far = list(range(half_dp, n_dp))
    near = list(range(1, half_dp))
    order = (far[0], far[1], *near[1:], *far[2:], near[0], 0)
    first = first_block(order[0], block, places, peer, wk, wv, gain, cosine, sine, own)
    kv, *blocks = peer_rows(order[1:], block, places, peer, wk, wv, gain, cosine, sine, own)
    first = swap(first, order[0])
    first, *blocks[4:-1] = lax.optimization_barrier((first, *blocks[4:-1]))
    received = [first] + [swap(a, k) for k, a in zip(order[1:], blocks)]
    attended = attend(prompt_offsets, queries, kv, block)
    cache = jax.ShapeDtypeStruct((n_dp * block, cols), jnp.bfloat16)
    anywhere = pl.BlockSpec(memory_space=pl.ANY)
    key_cache, value_cache = pl.pallas_call(
        functools.partial(gather_kernel, order, block),
        in_specs=[VMEM] * n_dp,
        out_specs=[anywhere] * 2,
        out_shape=[cache, cache],
        scratch_shapes=[pltpu.SemaphoreType.DMA((n_dp, 2))],
        compiler_params=pltpu.CompilerParams(vmem_limit_bytes=8 * MIB),
        name="place_blocks",
    )(*received)
    return attended, key_cache[None], value_cache[None]


def solution(mesh):
    rows = P(("groups", "dp"))
    in_specs = (
        P(("groups", "dp", "tensor"), None),
        P(),
        P(None, "tensor"),
        P(None, "tensor"),
        P(("groups", "dp"), "tensor"),
        rows, rows, rows, rows, rows,
    )
    out_specs = (
        P(("groups", "dp"), "tensor"),
        P(("groups", "dp"), None, "tensor"),
        P(("groups", "dp"), None, "tensor"),
    )
    return jax.shard_map(on_device, mesh=mesh, in_specs=in_specs, out_specs=out_specs, check_vma=False)
```

```python
import functools

import jax
import jax.numpy as jnp
import numpy as np
from jax import lax
from jax.experimental import pallas as pl
from jax.experimental.pallas import tpu as pltpu
from jax.sharding import PartitionSpec as P

HD = 128
EPSILON = 1e-05
ROPE_BASE = 500000.0
MIB = 1024 * 1024
SMEM = pl.BlockSpec(memory_space=pltpu.SMEM)
VMEM = pl.BlockSpec(memory_space=pltpu.VMEM)


def prompt_start(rows, offset_ref):
    start = jnp.zeros_like(rows)
    for s in range(offset_ref.shape[1]):
        offset = offset_ref[0, s]
        start = jnp.where(rows >= offset, jnp.maximum(start, offset), start)
    return start


def rotation_tables(block, offset_ref, cos_ref, sin_ref):
    position = lax.broadcasted_iota(jnp.int32, (block, HD), 0).astype(jnp.float32)
    lane = lax.broadcasted_iota(jnp.int32, (block, HD), 1)
    half = lax.broadcasted_iota(jnp.int32, (1, HD), 1) % (HD // 2)
    inverse = jnp.zeros((1, HD), jnp.float32)
    for i in range(HD // 2):
        inverse = jnp.where(half == i, np.float32(ROPE_BASE ** (-2.0 * i / HD)), inverse)
    angle = position * inverse
    cosine = jnp.cos(angle)
    sine = jnp.where(lane < HD // 2, -1.0, 1.0) * jnp.sin(angle)
    for s in range(offset_ref.shape[1]):
        rows = pl.ds(offset_ref[0, s], block)
        cos_ref[rows, :] = cosine
        sin_ref[rows, :] = sine


def project(h_ref, rows, gain_ref, wk_ref, wv_ref, acc_k, acc_v, squares, chunk, ready=None):
    for c in range(h_ref.shape[1] // chunk):
        if ready is not None:
            ready(c)
        at = slice(c * chunk, (c + 1) * chunk)
        h = h_ref[rows, at]
        scaled = h * gain_ref[:, at]
        key = jnp.dot(scaled, wk_ref[at, :], preferred_element_type=jnp.float32)
        value = jnp.dot(scaled, wv_ref[at, :], preferred_element_type=jnp.float32)
        parts = [h[:, j * HD : (j + 1) * HD].astype(jnp.float32) for j in range(chunk // HD)]
        total = sum(p * p for p in parts)
        if c == 0:
            acc_k[...], acc_v[...], squares[...] = key, value, total
        else:
            acc_k[...] += key
            acc_v[...] += value
            squares[...] += total


def finish(width, cosine, sine, acc_k, acc_v, squares):
    factor = lax.rsqrt(jnp.sum(squares[...], axis=1, keepdims=True) / width + EPSILON)
    keys = []
    for h in range(acc_k.shape[1] // HD):
        x = acc_k[:, h * HD : (h + 1) * HD] * factor
        keys.append((x * cosine + pltpu.roll(x, HD // 2, 1) * sine).astype(jnp.bfloat16))
    return jnp.concatenate(keys, axis=1), (acc_v[...] * factor).astype(jnp.bfloat16)


def own_kernel(
    block, chunk, offset_ref, h_hbm, wk_hbm, wv_hbm, gain_ref,
    out_ref, cos_ref, sin_ref, wk_ref, wv_ref, h_ref, acc_k, acc_v, squares, cos_pad, sin_pad, sems
):
    rows, width = h_hbm.shape
    cols = acc_k.shape[1]

    def copies(c):
        at = pl.ds(c * chunk, chunk)
        return (
            pltpu.make_async_copy(h_hbm.at[:, at], h_ref.at[:, at], sems.at[c, 0]),
            pltpu.make_async_copy(wk_hbm.at[at, :], wk_ref.at[at, :], sems.at[c, 1]),
            pltpu.make_async_copy(wv_hbm.at[at, :], wv_ref.at[at, :], sems.at[c, 2]),
        )

    def ready(c):
        for copy in copies(c):
            copy.wait()

    for c in range(width // chunk):
        for copy in copies(c):
            copy.start()
    rotation_tables(block, offset_ref, cos_pad, sin_pad)
    cos_ref[...] = cos_pad[: cos_ref.shape[0], :]
    sin_ref[...] = sin_pad[: sin_ref.shape[0], :]
    project(h_ref, slice(None), gain_ref, wk_ref, wv_ref, acc_k, acc_v, squares, chunk, ready)
    here = pl.ds(pl.multiple_of(lax.axis_index("tensor") * rows, rows), rows)
    keys, values = finish(width, cos_pad[here, :], sin_pad[here, :], acc_k, acc_v, squares)
    out_ref[:, :cols] = keys
    out_ref[:, cols:] = values


def own_rows(block, offsets, hidden, wk, wv, gain, tok_rows, chunk=1024):
    rows, width = hidden.shape
    cols = wk.shape[1]
    hbm = pl.BlockSpec(memory_space=pltpu.HBM)
    f32 = jnp.float32
    return pl.pallas_call(
        functools.partial(own_kernel, block, chunk),
        in_specs=[SMEM, hbm, hbm, hbm, VMEM],
        out_specs=[VMEM] * 5,
        out_shape=[
            jax.ShapeDtypeStruct((rows, 2 * cols), jnp.bfloat16),
            jax.ShapeDtypeStruct((tok_rows, HD), f32),
            jax.ShapeDtypeStruct((tok_rows, HD), f32),
            jax.ShapeDtypeStruct(wk.shape, wk.dtype),
            jax.ShapeDtypeStruct(wv.shape, wv.dtype),
        ],
        scratch_shapes=[
            pltpu.VMEM((rows, width), jnp.bfloat16),
            pltpu.VMEM((rows, cols), f32),
            pltpu.VMEM((rows, cols), f32),
            pltpu.VMEM((rows, HD), f32),
            pltpu.VMEM((tok_rows + block, HD), f32),
            pltpu.VMEM((tok_rows + block, HD), f32),
            pltpu.SemaphoreType.DMA((width // chunk, 3)),
        ],
        compiler_params=pltpu.CompilerParams(vmem_limit_bytes=44 * MIB),
        cost_estimate=pl.CostEstimate(
            flops=4 * rows * width * cols, bytes_accessed=2 * (rows * width + 2 * width * cols), transcendentals=0
        ),
        name="own_rows",
    )(offsets, hidden, wk, wv, gain)


def select_block(block, cols, owner, places, kv_ref, out_ref):
    offset_ref, length_ref, owner_ref, slot_ref = places
    offset = jnp.int32(0)
    length = jnp.int32(0)
    slot = jnp.int32(0)
    for s in range(owner_ref.shape[1]):
        hit = owner_ref[0, s] == owner
        offset = jnp.where(hit, offset_ref[0, s], offset)
        length = jnp.where(hit, length_ref[0, s], length)
        slot = jnp.where(hit, slot_ref[0, s], slot)
    span = block + 16
    start = jnp.minimum((offset // 16) * 16, kv_ref.shape[0] - span)
    start = pl.multiple_of(start, 16)
    place = lax.broadcasted_iota(jnp.int32, (block, span), 0) + (lax.axis_index("dp") * block - slot)
    token = lax.broadcasted_iota(jnp.int32, (block, span), 1) + (start - offset)
    chosen = (place == token) & (place >= 0) & (place < length)
    picked = jnp.dot(
        jnp.where(chosen, 1.0, 0.0).astype(jnp.bfloat16),
        kv_ref[pl.ds(start, span), :],
        preferred_element_type=jnp.float32,
    ).astype(jnp.bfloat16)
    out_ref[0] = picked[:, :cols]
    out_ref[1] = picked[:, cols:]


def first_kernel(
    owner, block, chunk, offset_ref, length_ref, owner_ref, slot_ref,
    h_ref, wk_ref, wv_ref, gain_ref, cos_ref, sin_ref, own_ref, block_ref, kv, acc_k, acc_v, squares
):
    rows, width = h_ref.shape
    cols = acc_k.shape[1]
    span = acc_k.shape[0]
    mine = lax.axis_index("tensor")
    owner = jnp.bitwise_xor(lax.axis_index("dp"), owner)
    here = pl.ds(pl.multiple_of(mine * rows, rows), rows)
    kv[here, :] = own_ref[...]
    offset = jnp.int32(0)
    for s in range(owner_ref.shape[1]):
        offset = jnp.where(owner_ref[0, s] == owner, offset_ref[0, s], offset)
    start = jnp.minimum((offset // 16) * 16, 2 * rows - span)
    local = pl.multiple_of(jnp.clip(start - (1 - mine) * rows, 0, rows - span), 16)
    there = pl.ds(pl.multiple_of((1 - mine) * rows + local, 16), span)
    project(h_ref, pl.ds(local, span), gain_ref, wk_ref, wv_ref, acc_k, acc_v, squares, chunk)
    keys, values = finish(width, cos_ref[there, :], sin_ref[there, :], acc_k, acc_v, squares)
    kv[there, :cols] = keys
    kv[there, cols:] = values
    select_block(block, cols, owner, (offset_ref, length_ref, owner_ref, slot_ref), kv, block_ref)


def first_block(owner, block, places, peer, wk, wv, gain, cosine, sine, own, chunk=1024):
    rows, width = peer.shape
    cols = wk.shape[1]
    span = block + 16
    return pl.pallas_call(
        functools.partial(first_kernel, owner, block, chunk),
        in_specs=[SMEM] * 4 + [VMEM] * 7,
        out_specs=VMEM,
        out_shape=jax.ShapeDtypeStruct((2, block, cols), jnp.bfloat16),
        scratch_shapes=[
            pltpu.VMEM((2 * rows, 2 * cols), jnp.bfloat16),
            pltpu.VMEM((span, cols), jnp.float32),
            pltpu.VMEM((span, cols), jnp.float32),
            pltpu.VMEM((span, HD), jnp.float32),
        ],
        compiler_params=pltpu.CompilerParams(vmem_limit_bytes=28 * MIB),
        cost_estimate=pl.CostEstimate(
            flops=4 * span * width * cols, bytes_accessed=2 * (span * width + 2 * width * cols), transcendentals=0
        ),
        name="first_block",
    )(*places, peer, wk, wv, gain, cosine, sine, own)


def peer_kernel(
    far, block, chunk, offset_ref, length_ref, owner_ref, slot_ref,
    h_ref, wk_ref, wv_ref, gain_ref, cos_ref, sin_ref, own_ref, kv_ref, *rest
):
    blocks, (acc_k, acc_v, squares) = rest[: len(far)], rest[len(far) :]
    rows, width = h_ref.shape
    cols = acc_k.shape[1]
    mine = lax.axis_index("tensor")
    there = pl.ds(pl.multiple_of((1 - mine) * rows, rows), rows)
    here = pl.ds(pl.multiple_of(mine * rows, rows), rows)
    project(h_ref, slice(None), gain_ref, wk_ref, wv_ref, acc_k, acc_v, squares, chunk)
    keys, values = finish(width, cos_ref[there, :], sin_ref[there, :], acc_k, acc_v, squares)
    kv_ref[there, :cols] = keys
    kv_ref[there, cols:] = values
    kv_ref[here, :] = own_ref[...]
    places = (offset_ref, length_ref, owner_ref, slot_ref)
    for k, out_ref in zip(far, blocks):
        select_block(block, cols, jnp.bitwise_xor(lax.axis_index("dp"), k), places, kv_ref, out_ref)


def peer_rows(far, block, places, peer, wk, wv, gain, cosine, sine, own, chunk=1024):
    rows, width = peer.shape
    cols = wk.shape[1]
    tok_rows = cosine.shape[0]
    return pl.pallas_call(
        functools.partial(peer_kernel, far, block, chunk),
        in_specs=[SMEM] * 4 + [VMEM] * 7,
        out_specs=[VMEM] * (1 + len(far)),
        out_shape=[jax.ShapeDtypeStruct((tok_rows, 2 * cols), jnp.bfloat16)]
        + [jax.ShapeDtypeStruct((2, block, cols), jnp.bfloat16)] * len(far),
        scratch_shapes=[
            pltpu.VMEM((rows, cols), jnp.float32),
            pltpu.VMEM((rows, cols), jnp.float32),
            pltpu.VMEM((rows, HD), jnp.float32),
        ],
        compiler_params=pltpu.CompilerParams(vmem_limit_bytes=28 * MIB),
        cost_estimate=pl.CostEstimate(
            flops=4 * rows * width * cols, bytes_accessed=2 * (rows * width + 2 * width * cols), transcendentals=0
        ),
        name="peer_rows",
    )(*places, peer, wk, wv, gain, cosine, sine, own)


def attend_kernel(tile, window, offset_ref, q_ref, kv_ref, out_ref):
    cols = kv_ref.shape[1] // 2
    groups = cols // HD
    heads = q_ref.shape[1] // HD // groups
    first = pl.program_id(0) * tile
    start = pl.multiple_of(jnp.maximum(first + tile - window, 0), 16)
    row = first + lax.broadcasted_iota(jnp.int32, (tile, window), 0)
    key = start + lax.broadcasted_iota(jnp.int32, (tile, window), 1)
    allowed = (key <= row) & (key >= prompt_start(row, offset_ref))
    bias = jnp.where(allowed, 0.0, -1e30)[None]
    ones = jnp.ones((window, HD), jnp.bfloat16)
    scale = HD**-0.5 * float(np.log2(np.e))
    for g in range(groups):
        at = [slice((g * heads + h) * HD, (g * heads + h + 1) * HD) for h in range(heads)]
        q = jnp.concatenate([q_ref[:, a] for a in at], axis=0)
        k = kv_ref[pl.ds(start, window), g * HD : (g + 1) * HD]
        v = kv_ref[pl.ds(start, window), cols + g * HD : cols + (g + 1) * HD]
        scores = lax.dot_general(q, k, (((1,), (1,)), ((), ())), preferred_element_type=jnp.float32)
        scores = scores.reshape(heads, tile, window) * scale + bias
        exponent = jnp.exp2(scores - jnp.max(scores, axis=2, keepdims=True))
        exponent = exponent.astype(jnp.bfloat16).reshape(heads * tile, window)
        summed = jnp.dot(exponent, jnp.concatenate([v, ones], axis=1), preferred_element_type=jnp.float32)
        result = (summed[:, :HD] / summed[:, HD:]).astype(jnp.bfloat16)
        for h, a in enumerate(at):
            out_ref[:, a] = result[h * tile : (h + 1) * tile]


def attend(offsets, queries, kv, longest, tile=64):
    rows, width = queries.shape
    window = tile + longest
    rows_at = pl.BlockSpec((tile, width), lambda i: (i, 0))
    return pl.pallas_call(
        functools.partial(attend_kernel, tile, window),
        grid=(rows // tile,),
        in_specs=[SMEM, rows_at, pl.BlockSpec(kv.shape, lambda i: (0, 0))],
        out_specs=rows_at,
        out_shape=jax.ShapeDtypeStruct((rows, width), jnp.bfloat16),
        compiler_params=pltpu.CompilerParams(vmem_limit_bytes=32 * MIB),
        cost_estimate=pl.CostEstimate(
            flops=4 * rows * width * window,
            bytes_accessed=4 * rows * width,
            transcendentals=rows * window * width // HD,
        ),
        name="attend",
    )(offsets, queries, kv)


def gather_kernel(order, block, *refs):
    key_ref, value_ref, sems = refs[-3:]
    me = lax.axis_index("dp")
    copies = []
    for i, k in enumerate(order):
        rows = pl.ds(pl.multiple_of(jnp.bitwise_xor(me, k) * block, block), block)
        for n, out_ref in enumerate((key_ref, value_ref)):
            copies.append(pltpu.make_async_copy(refs[i].at[n], out_ref.at[rows, :], sems.at[i, n]))
    for copy in copies:
        copy.start()
    for copy in copies:
        copy.wait()


def place(order, block, blocks, cache, before=()):
    n = len(order)
    anywhere = pl.BlockSpec(memory_space=pl.ANY)
    return pl.pallas_call(
        functools.partial(gather_kernel, order, block),
        in_specs=[VMEM] * n + [anywhere] * len(before),
        out_specs=[anywhere] * 2,
        out_shape=[cache, cache],
        input_output_aliases={n: 0, n + 1: 1} if before else {},
        scratch_shapes=[pltpu.SemaphoreType.DMA((n, 2))],
        compiler_params=pltpu.CompilerParams(vmem_limit_bytes=8 * MIB),
        name="place_rest" if before else "place_first",
    )(*blocks, *before)


def on_device(
    hidden, norm_gain, key_weight, value_weight, queries,
    segment_ids, prompt_lengths, prompt_offsets, decode_owner, slot_offsets,
):
    n_dp = lax.axis_size("dp")
    half, width = hidden.shape
    tok_rows = queries.shape[0]
    cols = key_weight.shape[1]
    block = 2 * tok_rows // n_dp
    gain = norm_gain.reshape(1, width)

    peer = lax.ppermute(hidden, "tensor", [(0, 1), (1, 0)])
    own, cosine, sine, wk, wv = own_rows(
        block, prompt_offsets, hidden, key_weight, value_weight, gain, tok_rows
    )
    places = [prompt_offsets, prompt_lengths, decode_owner, slot_offsets]
    swap = lambda a, k: lax.ppermute(a, "dp", [(p, p ^ k) for p in range(n_dp)]) if k else a
    half_dp = n_dp // 2
    far = list(range(half_dp, n_dp))
    near = list(range(1, half_dp))
    order = (far[2], far[1], *near[1:], far[0], *far[3:], near[0], 0)
    first = first_block(order[0], block, places, peer, wk, wv, gain, cosine, sine, own)
    kv, *blocks = peer_rows(order[1:], block, places, peer, wk, wv, gain, cosine, sine, own)
    first = swap(first, order[0])
    first, *blocks[4:-1] = lax.optimization_barrier((first, *blocks[4:-1]))
    received = [first] + [swap(a, k) for k, a in zip(order[1:], blocks)]
    attended = attend(prompt_offsets, queries, kv, block)
    cache = jax.ShapeDtypeStruct((n_dp * block, cols), jnp.bfloat16)
    by_place = dict(zip(order, received))
    early = (0, *order[: n_dp // 2 + 1])
    late = tuple(k for k in order if k not in early)
    caches = place(early, block, [by_place[k] for k in early], cache)
    key_cache, value_cache = place(late, block, [by_place[k] for k in late], cache, caches)
    return attended, key_cache[None], value_cache[None]


def solution(mesh):
    rows = P(("groups", "dp"))
    in_specs = (
        P(("groups", "dp", "tensor"), None),
        P(),
        P(None, "tensor"),
        P(None, "tensor"),
        P(("groups", "dp"), "tensor"),
        rows, rows, rows, rows, rows,
    )
    out_specs = (
        P(("groups", "dp"), "tensor"),
        P(("groups", "dp"), None, "tensor"),
        P(("groups", "dp"), None, "tensor"),
    )
    return jax.shard_map(on_device, mesh=mesh, in_specs=in_specs, out_specs=out_specs, check_vma=False)
```

```python
import functools

import jax
import jax.numpy as jnp
import numpy as np
from jax import lax
from jax.experimental import pallas as pl
from jax.experimental.pallas import tpu as pltpu
from jax.sharding import PartitionSpec as P

HD = 128
EPSILON = 1e-05
ROPE_BASE = 500000.0
MIB = 1024 * 1024
SMEM = pl.BlockSpec(memory_space=pltpu.SMEM)
VMEM = pl.BlockSpec(memory_space=pltpu.VMEM)


def prompt_start(rows, offset_ref):
    start = jnp.zeros_like(rows)
    for s in range(offset_ref.shape[1]):
        offset = offset_ref[0, s]
        start = jnp.where(rows >= offset, jnp.maximum(start, offset), start)
    return start


def rotation_tables(block, offset_ref, cos_ref, sin_ref):
    position = lax.broadcasted_iota(jnp.int32, (block, HD), 0).astype(jnp.float32)
    lane = lax.broadcasted_iota(jnp.int32, (block, HD), 1)
    half = lax.broadcasted_iota(jnp.int32, (1, HD), 1) % (HD // 2)
    inverse = jnp.zeros((1, HD), jnp.float32)
    for i in range(HD // 2):
        inverse = jnp.where(half == i, np.float32(ROPE_BASE ** (-2.0 * i / HD)), inverse)
    angle = position * inverse
    cosine = jnp.cos(angle)
    sine = jnp.where(lane < HD // 2, -1.0, 1.0) * jnp.sin(angle)
    for s in range(offset_ref.shape[1]):
        rows = pl.ds(offset_ref[0, s], block)
        cos_ref[rows, :] = cosine
        sin_ref[rows, :] = sine


def project(h_ref, rows, gain_ref, wk_ref, wv_ref, acc_k, acc_v, squares, chunk, ready=None, loaded=None):
    width = h_ref.shape[1]
    for c in range(width // chunk):
        if ready is not None:
            ready(c)
        h = h_ref[rows, c * chunk : (c + 1) * chunk]
        parts = [h[:, j * HD : (j + 1) * HD].astype(jnp.float32) for j in range(chunk // HD)]
        total = sum(p * p for p in parts)
        squares[...] = total if c == 0 else squares[...] + total
    factor = lax.rsqrt(jnp.sum(squares[...], axis=1, keepdims=True) / width + EPSILON)
    for c in range(width // chunk):
        if loaded is not None:
            loaded(c)
        at = slice(c * chunk, (c + 1) * chunk)
        normed = h_ref[rows, at].astype(jnp.float32) * factor * gain_ref[:, at].astype(jnp.float32)
        normed = normed.astype(jnp.bfloat16)
        for w_ref, acc in ((wk_ref, acc_k), (wv_ref, acc_v)):
            product = jnp.dot(normed, w_ref[at, :], preferred_element_type=jnp.float32)
            acc[...] = product if c == 0 else acc[...] + product


def finish(cosine, sine, acc_k, acc_v):
    keys = []
    for h in range(acc_k.shape[1] // HD):
        x = acc_k[:, h * HD : (h + 1) * HD]
        keys.append((x * cosine + pltpu.roll(x, HD // 2, 1) * sine).astype(jnp.bfloat16))
    return jnp.concatenate(keys, axis=1), acc_v[...].astype(jnp.bfloat16)


def own_kernel(
    block, chunk, offset_ref, h_hbm, wk_hbm, wv_hbm, gain_ref,
    out_ref, cos_ref, sin_ref, wk_ref, wv_ref, h_ref, acc_k, acc_v, squares, cos_pad, sin_pad, sems
):
    rows, width = h_hbm.shape
    cols = acc_k.shape[1]

    def copies(c):
        at = pl.ds(c * chunk, chunk)
        return (
            pltpu.make_async_copy(h_hbm.at[:, at], h_ref.at[:, at], sems.at[c, 0]),
            pltpu.make_async_copy(wk_hbm.at[at, :], wk_ref.at[at, :], sems.at[c, 1]),
            pltpu.make_async_copy(wv_hbm.at[at, :], wv_ref.at[at, :], sems.at[c, 2]),
        )

    def ready(c):
        copies(c)[0].wait()

    def loaded(c):
        for copy in copies(c)[1:]:
            copy.wait()

    for c in range(width // chunk):
        copies(c)[0].start()
    for c in range(width // chunk):
        for copy in copies(c)[1:]:
            copy.start()
    rotation_tables(block, offset_ref, cos_pad, sin_pad)
    cos_ref[...] = cos_pad[: cos_ref.shape[0], :]
    sin_ref[...] = sin_pad[: sin_ref.shape[0], :]
    project(h_ref, slice(None), gain_ref, wk_ref, wv_ref, acc_k, acc_v, squares, chunk, ready, loaded)
    here = pl.ds(pl.multiple_of(lax.axis_index("tensor") * rows, rows), rows)
    keys, values = finish(cos_pad[here, :], sin_pad[here, :], acc_k, acc_v)
    out_ref[:, :cols] = keys
    out_ref[:, cols:] = values


def own_rows(block, offsets, hidden, wk, wv, gain, tok_rows, chunk=1024):
    rows, width = hidden.shape
    cols = wk.shape[1]
    hbm = pl.BlockSpec(memory_space=pltpu.HBM)
    f32 = jnp.float32
    return pl.pallas_call(
        functools.partial(own_kernel, block, chunk),
        in_specs=[SMEM, hbm, hbm, hbm, VMEM],
        out_specs=[VMEM] * 5,
        out_shape=[
            jax.ShapeDtypeStruct((rows, 2 * cols), jnp.bfloat16),
            jax.ShapeDtypeStruct((tok_rows, HD), f32),
            jax.ShapeDtypeStruct((tok_rows, HD), f32),
            jax.ShapeDtypeStruct(wk.shape, wk.dtype),
            jax.ShapeDtypeStruct(wv.shape, wv.dtype),
        ],
        scratch_shapes=[
            pltpu.VMEM((rows, width), jnp.bfloat16),
            pltpu.VMEM((rows, cols), f32),
            pltpu.VMEM((rows, cols), f32),
            pltpu.VMEM((rows, HD), f32),
            pltpu.VMEM((tok_rows + block, HD), f32),
            pltpu.VMEM((tok_rows + block, HD), f32),
            pltpu.SemaphoreType.DMA((width // chunk, 3)),
        ],
        compiler_params=pltpu.CompilerParams(vmem_limit_bytes=44 * MIB),
        cost_estimate=pl.CostEstimate(
            flops=4 * rows * width * cols, bytes_accessed=2 * (rows * width + 2 * width * cols), transcendentals=0
        ),
        name="own_rows",
    )(offsets, hidden, wk, wv, gain)


def select_block(block, cols, owner, places, kv_ref, out_ref):
    offset_ref, length_ref, owner_ref, slot_ref = places
    offset = jnp.int32(0)
    length = jnp.int32(0)
    slot = jnp.int32(0)
    for s in range(owner_ref.shape[1]):
        hit = owner_ref[0, s] == owner
        offset = jnp.where(hit, offset_ref[0, s], offset)
        length = jnp.where(hit, length_ref[0, s], length)
        slot = jnp.where(hit, slot_ref[0, s], slot)
    span = block + 16
    start = jnp.minimum((offset // 16) * 16, kv_ref.shape[0] - span)
    start = pl.multiple_of(start, 16)
    place = lax.broadcasted_iota(jnp.int32, (block, span), 0) + (lax.axis_index("dp") * block - slot)
    token = lax.broadcasted_iota(jnp.int32, (block, span), 1) + (start - offset)
    chosen = (place == token) & (place >= 0) & (place < length)
    picked = jnp.dot(
        jnp.where(chosen, 1.0, 0.0).astype(jnp.bfloat16),
        kv_ref[pl.ds(start, span), :],
        preferred_element_type=jnp.float32,
    ).astype(jnp.bfloat16)
    out_ref[0] = picked[:, :cols]
    out_ref[1] = picked[:, cols:]


def first_kernel(
    owner, block, chunk, offset_ref, length_ref, owner_ref, slot_ref,
    h_ref, wk_ref, wv_ref, gain_ref, cos_ref, sin_ref, own_ref, block_ref, kv, acc_k, acc_v, squares
):
    rows, width = h_ref.shape
    cols = acc_k.shape[1]
    span = acc_k.shape[0]
    mine = lax.axis_index("tensor")
    owner = jnp.bitwise_xor(lax.axis_index("dp"), owner)
    here = pl.ds(pl.multiple_of(mine * rows, rows), rows)
    kv[here, :] = own_ref[...]
    offset = jnp.int32(0)
    for s in range(owner_ref.shape[1]):
        offset = jnp.where(owner_ref[0, s] == owner, offset_ref[0, s], offset)
    start = jnp.minimum((offset // 16) * 16, 2 * rows - span)
    local = pl.multiple_of(jnp.clip(start - (1 - mine) * rows, 0, rows - span), 16)
    there = pl.ds(pl.multiple_of((1 - mine) * rows + local, 16), span)
    project(h_ref, pl.ds(local, span), gain_ref, wk_ref, wv_ref, acc_k, acc_v, squares, chunk)
    keys, values = finish(cos_ref[there, :], sin_ref[there, :], acc_k, acc_v)
    kv[there, :cols] = keys
    kv[there, cols:] = values
    select_block(block, cols, owner, (offset_ref, length_ref, owner_ref, slot_ref), kv, block_ref)


def first_block(owner, block, places, peer, wk, wv, gain, cosine, sine, own, chunk=1024):
    rows, width = peer.shape
    cols = wk.shape[1]
    span = block + 16
    return pl.pallas_call(
        functools.partial(first_kernel, owner, block, chunk),
        in_specs=[SMEM] * 4 + [VMEM] * 7,
        out_specs=VMEM,
        out_shape=jax.ShapeDtypeStruct((2, block, cols), jnp.bfloat16),
        scratch_shapes=[
            pltpu.VMEM((2 * rows, 2 * cols), jnp.bfloat16),
            pltpu.VMEM((span, cols), jnp.float32),
            pltpu.VMEM((span, cols), jnp.float32),
            pltpu.VMEM((span, HD), jnp.float32),
        ],
        compiler_params=pltpu.CompilerParams(vmem_limit_bytes=28 * MIB),
        cost_estimate=pl.CostEstimate(
            flops=4 * span * width * cols, bytes_accessed=2 * (span * width + 2 * width * cols), transcendentals=0
        ),
        name="first_block",
    )(*places, peer, wk, wv, gain, cosine, sine, own)


def peer_kernel(
    far, block, chunk, offset_ref, length_ref, owner_ref, slot_ref,
    h_ref, wk_ref, wv_ref, gain_ref, cos_ref, sin_ref, own_ref, kv_ref, *rest
):
    blocks, (acc_k, acc_v, squares) = rest[: len(far)], rest[len(far) :]
    rows, width = h_ref.shape
    cols = acc_k.shape[1]
    mine = lax.axis_index("tensor")
    there = pl.ds(pl.multiple_of((1 - mine) * rows, rows), rows)
    here = pl.ds(pl.multiple_of(mine * rows, rows), rows)
    project(h_ref, slice(None), gain_ref, wk_ref, wv_ref, acc_k, acc_v, squares, chunk)
    keys, values = finish(cos_ref[there, :], sin_ref[there, :], acc_k, acc_v)
    kv_ref[there, :cols] = keys
    kv_ref[there, cols:] = values
    kv_ref[here, :] = own_ref[...]
    places = (offset_ref, length_ref, owner_ref, slot_ref)
    for k, out_ref in zip(far, blocks):
        select_block(block, cols, jnp.bitwise_xor(lax.axis_index("dp"), k), places, kv_ref, out_ref)


def peer_rows(far, block, places, peer, wk, wv, gain, cosine, sine, own, chunk=1024):
    rows, width = peer.shape
    cols = wk.shape[1]
    tok_rows = cosine.shape[0]
    return pl.pallas_call(
        functools.partial(peer_kernel, far, block, chunk),
        in_specs=[SMEM] * 4 + [VMEM] * 7,
        out_specs=[VMEM] * (1 + len(far)),
        out_shape=[jax.ShapeDtypeStruct((tok_rows, 2 * cols), jnp.bfloat16)]
        + [jax.ShapeDtypeStruct((2, block, cols), jnp.bfloat16)] * len(far),
        scratch_shapes=[
            pltpu.VMEM((rows, cols), jnp.float32),
            pltpu.VMEM((rows, cols), jnp.float32),
            pltpu.VMEM((rows, HD), jnp.float32),
        ],
        compiler_params=pltpu.CompilerParams(vmem_limit_bytes=28 * MIB),
        cost_estimate=pl.CostEstimate(
            flops=4 * rows * width * cols, bytes_accessed=2 * (rows * width + 2 * width * cols), transcendentals=0
        ),
        name="peer_rows",
    )(*places, peer, wk, wv, gain, cosine, sine, own)


def attend_kernel(tile, window, offset_ref, q_ref, kv_ref, out_ref):
    cols = kv_ref.shape[1] // 2
    groups = cols // HD
    heads = q_ref.shape[1] // HD // groups
    first = pl.program_id(0) * tile
    start = pl.multiple_of(jnp.maximum(first + tile - window, 0), 16)
    row = first + lax.broadcasted_iota(jnp.int32, (tile, window), 0)
    key = start + lax.broadcasted_iota(jnp.int32, (tile, window), 1)
    allowed = (key <= row) & (key >= prompt_start(row, offset_ref))
    bias = jnp.where(allowed, 0.0, -1e30)[None]
    ones = jnp.ones((window, HD), jnp.bfloat16)
    scale = HD**-0.5 * float(np.log2(np.e))
    for g in range(groups):
        at = [slice((g * heads + h) * HD, (g * heads + h + 1) * HD) for h in range(heads)]
        q = jnp.concatenate([q_ref[:, a] for a in at], axis=0)
        k = kv_ref[pl.ds(start, window), g * HD : (g + 1) * HD]
        v = kv_ref[pl.ds(start, window), cols + g * HD : cols + (g + 1) * HD]
        scores = lax.dot_general(q, k, (((1,), (1,)), ((), ())), preferred_element_type=jnp.float32)
        scores = scores.reshape(heads, tile, window) * scale + bias
        exponent = jnp.exp2(scores - jnp.max(scores, axis=2, keepdims=True))
        exponent = exponent.astype(jnp.bfloat16).reshape(heads * tile, window)
        summed = jnp.dot(exponent, jnp.concatenate([v, ones], axis=1), preferred_element_type=jnp.float32)
        result = (summed[:, :HD] / summed[:, HD:]).astype(jnp.bfloat16)
        for h, a in enumerate(at):
            out_ref[:, a] = result[h * tile : (h + 1) * tile]


def attend(offsets, queries, kv, longest, tile=64):
    rows, width = queries.shape
    window = tile + longest
    rows_at = pl.BlockSpec((tile, width), lambda i: (i, 0))
    return pl.pallas_call(
        functools.partial(attend_kernel, tile, window),
        grid=(rows // tile,),
        in_specs=[SMEM, rows_at, pl.BlockSpec(kv.shape, lambda i: (0, 0))],
        out_specs=rows_at,
        out_shape=jax.ShapeDtypeStruct((rows, width), jnp.bfloat16),
        compiler_params=pltpu.CompilerParams(vmem_limit_bytes=32 * MIB),
        cost_estimate=pl.CostEstimate(
            flops=4 * rows * width * window,
            bytes_accessed=4 * rows * width,
            transcendentals=rows * window * width // HD,
        ),
        name="attend",
    )(offsets, queries, kv)


def gather_kernel(order, block, *refs):
    key_ref, value_ref, sems = refs[-3:]
    me = lax.axis_index("dp")
    copies = []
    for i, k in enumerate(order):
        rows = pl.ds(pl.multiple_of(jnp.bitwise_xor(me, k) * block, block), block)
        for n, out_ref in enumerate((key_ref, value_ref)):
            copies.append(pltpu.make_async_copy(refs[i].at[n], out_ref.at[rows, :], sems.at[i, n]))
    for copy in copies:
        copy.start()
    for copy in copies:
        copy.wait()


def place(order, block, blocks, cache, before=()):
    n = len(order)
    anywhere = pl.BlockSpec(memory_space=pl.ANY)
    return pl.pallas_call(
        functools.partial(gather_kernel, order, block),
        in_specs=[VMEM] * n + [anywhere] * len(before),
        out_specs=[anywhere] * 2,
        out_shape=[cache, cache],
        input_output_aliases={n: 0, n + 1: 1} if before else {},
        scratch_shapes=[pltpu.SemaphoreType.DMA((n, 2))],
        compiler_params=pltpu.CompilerParams(vmem_limit_bytes=8 * MIB),
        name="place_rest" if before else "place_first",
    )(*blocks, *before)


def on_device(
    hidden, norm_gain, key_weight, value_weight, queries,
    segment_ids, prompt_lengths, prompt_offsets, decode_owner, slot_offsets,
):
    n_dp = lax.axis_size("dp")
    half, width = hidden.shape
    tok_rows = queries.shape[0]
    cols = key_weight.shape[1]
    block = 2 * tok_rows // n_dp
    gain = norm_gain.reshape(1, width)

    peer = lax.ppermute(hidden, "tensor", [(0, 1), (1, 0)])
    own, cosine, sine, wk, wv = own_rows(
        block, prompt_offsets, hidden, key_weight, value_weight, gain, tok_rows
    )
    places = [prompt_offsets, prompt_lengths, decode_owner, slot_offsets]
    swap = lambda a, k: lax.ppermute(a, "dp", [(p, p ^ k) for p in range(n_dp)]) if k else a
    half_dp = n_dp // 2
    far = list(range(half_dp, n_dp))
    near = list(range(1, half_dp))
    order = (far[2], far[1], *near[1:], far[0], *far[3:], near[0], 0)
    first = first_block(order[0], block, places, peer, wk, wv, gain, cosine, sine, own)
    kv, *blocks = peer_rows(order[1:], block, places, peer, wk, wv, gain, cosine, sine, own)
    first = swap(first, order[0])
    first, *blocks[4:-1] = lax.optimization_barrier((first, *blocks[4:-1]))
    received = [first] + [swap(a, k) for k, a in zip(order[1:], blocks)]
    attended = attend(prompt_offsets, queries, kv, block)
    cache = jax.ShapeDtypeStruct((n_dp * block, cols), jnp.bfloat16)
    by_place = dict(zip(order, received))
    early = (0, *order[: n_dp // 2 + 1])
    late = tuple(k for k in order if k not in early)
    caches = place(early, block, [by_place[k] for k in early], cache)
    key_cache, value_cache = place(late, block, [by_place[k] for k in late], cache, caches)
    return attended, key_cache[None], value_cache[None]


def solution(mesh):
    rows = P(("groups", "dp"))
    in_specs = (
        P(("groups", "dp", "tensor"), None),
        P(),
        P(None, "tensor"),
        P(None, "tensor"),
        P(("groups", "dp"), "tensor"),
        rows, rows, rows, rows, rows,
    )
    out_specs = (
        P(("groups", "dp"), "tensor"),
        P(("groups", "dp"), None, "tensor"),
        P(("groups", "dp"), None, "tensor"),
    )
    return jax.shard_map(on_device, mesh=mesh, in_specs=in_specs, out_specs=out_specs, check_vma=False)
```

```python
import functools

import jax
import jax.numpy as jnp
import numpy as np
from jax import lax
from jax.experimental import pallas as pl
from jax.experimental.pallas import tpu as pltpu
from jax.sharding import PartitionSpec as P

HD = 128
EPSILON = 1e-05
ROPE_BASE = 500000.0
MIB = 1024 * 1024
SMEM = pl.BlockSpec(memory_space=pltpu.SMEM)
VMEM = pl.BlockSpec(memory_space=pltpu.VMEM)


def prompt_start(rows, offset_ref):
    start = jnp.zeros_like(rows)
    for s in range(offset_ref.shape[1]):
        offset = offset_ref[0, s]
        start = jnp.where(rows >= offset, jnp.maximum(start, offset), start)
    return start


def rotation_tables(block, offset_ref, cos_ref, sin_ref):
    position = lax.broadcasted_iota(jnp.int32, (block, HD), 0).astype(jnp.float32)
    lane = lax.broadcasted_iota(jnp.int32, (block, HD), 1)
    half = lax.broadcasted_iota(jnp.int32, (1, HD), 1) % (HD // 2)
    inverse = jnp.zeros((1, HD), jnp.float32)
    for i in range(HD // 2):
        inverse = jnp.where(half == i, np.float32(ROPE_BASE ** (-2.0 * i / HD)), inverse)
    angle = position * inverse
    cosine = jnp.cos(angle)
    sine = jnp.where(lane < HD // 2, -1.0, 1.0) * jnp.sin(angle)
    for s in range(offset_ref.shape[1]):
        rows = pl.ds(offset_ref[0, s], block)
        cos_ref[rows, :] = cosine
        sin_ref[rows, :] = sine


def norm_factor(h_ref, rows, squares, chunk, ready=None):
    width = h_ref.shape[1]
    for c in range(width // chunk):
        if ready is not None:
            ready(c)
        h = h_ref[rows, c * chunk : (c + 1) * chunk]
        parts = [h[:, j * HD : (j + 1) * HD].astype(jnp.float32) for j in range(chunk // HD)]
        total = sum(p * p for p in parts)
        squares[...] = total if c == 0 else squares[...] + total
    return lax.rsqrt(jnp.sum(squares[...], axis=1, keepdims=True) / width + EPSILON)


def project(h_ref, rows, gain_ref, wk_ref, wv_ref, acc_k, acc_v, factor, chunk, loaded=None):
    width = h_ref.shape[1]
    for c in range(width // chunk):
        if loaded is not None:
            loaded(c)
        at = slice(c * chunk, (c + 1) * chunk)
        normed = h_ref[rows, at].astype(jnp.float32) * factor * gain_ref[:, at].astype(jnp.float32)
        normed = normed.astype(jnp.bfloat16)
        for w_ref, acc in ((wk_ref, acc_k), (wv_ref, acc_v)):
            product = jnp.dot(normed, w_ref[at, :], preferred_element_type=jnp.float32)
            acc[...] = product if c == 0 else acc[...] + product


def finish(cosine, sine, acc_k, acc_v):
    keys = []
    for h in range(acc_k.shape[1] // HD):
        x = acc_k[:, h * HD : (h + 1) * HD]
        keys.append((x * cosine + pltpu.roll(x, HD // 2, 1) * sine).astype(jnp.bfloat16))
    return jnp.concatenate(keys, axis=1), acc_v[...].astype(jnp.bfloat16)


def own_kernel(
    block, chunk, offset_ref, h_hbm, wk_hbm, wv_hbm, gain_ref,
    out_ref, factor_ref, cos_ref, sin_ref, wk_ref, wv_ref, h_ref, acc_k, acc_v, squares, cos_pad, sin_pad, sems
):
    rows, width = h_hbm.shape
    cols = acc_k.shape[1]

    def copies(c):
        at = pl.ds(c * chunk, chunk)
        return (
            pltpu.make_async_copy(h_hbm.at[:, at], h_ref.at[:, at], sems.at[c, 0]),
            pltpu.make_async_copy(wk_hbm.at[at, :], wk_ref.at[at, :], sems.at[c, 1]),
            pltpu.make_async_copy(wv_hbm.at[at, :], wv_ref.at[at, :], sems.at[c, 2]),
        )

    def ready(c):
        copies(c)[0].wait()

    def loaded(c):
        for copy in copies(c)[1:]:
            copy.wait()

    for c in range(width // chunk):
        copies(c)[0].start()
    for c in range(width // chunk):
        for copy in copies(c)[1:]:
            copy.start()
    rotation_tables(block, offset_ref, cos_pad, sin_pad)
    cos_ref[...] = cos_pad[: cos_ref.shape[0], :]
    sin_ref[...] = sin_pad[: sin_ref.shape[0], :]
    factor = norm_factor(h_ref, slice(None), squares, chunk, ready)
    factor_ref[...] = jnp.broadcast_to(factor, factor_ref.shape)
    project(h_ref, slice(None), gain_ref, wk_ref, wv_ref, acc_k, acc_v, factor, chunk, loaded)
    here = pl.ds(pl.multiple_of(lax.axis_index("tensor") * rows, rows), rows)
    keys, values = finish(cos_pad[here, :], sin_pad[here, :], acc_k, acc_v)
    out_ref[:, :cols] = keys
    out_ref[:, cols:] = values


def own_rows(block, offsets, hidden, wk, wv, gain, tok_rows, chunk=1024):
    rows, width = hidden.shape
    cols = wk.shape[1]
    hbm = pl.BlockSpec(memory_space=pltpu.HBM)
    f32 = jnp.float32
    return pl.pallas_call(
        functools.partial(own_kernel, block, chunk),
        in_specs=[SMEM, hbm, hbm, hbm, VMEM],
        out_specs=[VMEM] * 6,
        out_shape=[
            jax.ShapeDtypeStruct((rows, 2 * cols), jnp.bfloat16),
            jax.ShapeDtypeStruct((rows, HD), f32),
            jax.ShapeDtypeStruct((tok_rows, HD), f32),
            jax.ShapeDtypeStruct((tok_rows, HD), f32),
            jax.ShapeDtypeStruct(wk.shape, wk.dtype),
            jax.ShapeDtypeStruct(wv.shape, wv.dtype),
        ],
        scratch_shapes=[
            pltpu.VMEM((rows, width), jnp.bfloat16),
            pltpu.VMEM((rows, cols), f32),
            pltpu.VMEM((rows, cols), f32),
            pltpu.VMEM((rows, HD), f32),
            pltpu.VMEM((tok_rows + block, HD), f32),
            pltpu.VMEM((tok_rows + block, HD), f32),
            pltpu.SemaphoreType.DMA((width // chunk, 3)),
        ],
        compiler_params=pltpu.CompilerParams(vmem_limit_bytes=44 * MIB),
        cost_estimate=pl.CostEstimate(
            flops=4 * rows * width * cols, bytes_accessed=2 * (rows * width + 2 * width * cols), transcendentals=0
        ),
        name="own_rows",
    )(offsets, hidden, wk, wv, gain)


def select_block(block, cols, owner, places, kv_ref, out_ref):
    offset_ref, length_ref, owner_ref, slot_ref = places
    offset = jnp.int32(0)
    length = jnp.int32(0)
    slot = jnp.int32(0)
    for s in range(owner_ref.shape[1]):
        hit = owner_ref[0, s] == owner
        offset = jnp.where(hit, offset_ref[0, s], offset)
        length = jnp.where(hit, length_ref[0, s], length)
        slot = jnp.where(hit, slot_ref[0, s], slot)
    span = block + 16
    start = jnp.minimum((offset // 16) * 16, kv_ref.shape[0] - span)
    start = pl.multiple_of(start, 16)
    place = lax.broadcasted_iota(jnp.int32, (block, span), 0) + (lax.axis_index("dp") * block - slot)
    token = lax.broadcasted_iota(jnp.int32, (block, span), 1) + (start - offset)
    chosen = (place == token) & (place >= 0) & (place < length)
    picked = jnp.dot(
        jnp.where(chosen, 1.0, 0.0).astype(jnp.bfloat16),
        kv_ref[pl.ds(start, span), :],
        preferred_element_type=jnp.float32,
    ).astype(jnp.bfloat16)
    out_ref[0] = picked[:, :cols]
    out_ref[1] = picked[:, cols:]


def first_kernel(
    owner, block, chunk, offset_ref, length_ref, owner_ref, slot_ref,
    h_ref, wk_ref, wv_ref, gain_ref, cos_ref, sin_ref, own_ref, block_ref, kv, acc_k, acc_v, squares
):
    rows, width = h_ref.shape
    cols = acc_k.shape[1]
    span = acc_k.shape[0]
    mine = lax.axis_index("tensor")
    owner = jnp.bitwise_xor(lax.axis_index("dp"), owner)
    here = pl.ds(pl.multiple_of(mine * rows, rows), rows)
    kv[here, :] = own_ref[...]
    offset = jnp.int32(0)
    for s in range(owner_ref.shape[1]):
        offset = jnp.where(owner_ref[0, s] == owner, offset_ref[0, s], offset)
    start = jnp.minimum((offset // 16) * 16, 2 * rows - span)
    local = pl.multiple_of(jnp.clip(start - (1 - mine) * rows, 0, rows - span), 16)
    there = pl.ds(pl.multiple_of((1 - mine) * rows + local, 16), span)
    factor = norm_factor(h_ref, pl.ds(local, span), squares, chunk)
    project(h_ref, pl.ds(local, span), gain_ref, wk_ref, wv_ref, acc_k, acc_v, factor, chunk)
    keys, values = finish(cos_ref[there, :], sin_ref[there, :], acc_k, acc_v)
    kv[there, :cols] = keys
    kv[there, cols:] = values
    select_block(block, cols, owner, (offset_ref, length_ref, owner_ref, slot_ref), kv, block_ref)


def first_block(owner, block, places, peer, wk, wv, gain, cosine, sine, own, chunk=1024):
    rows, width = peer.shape
    cols = wk.shape[1]
    span = block + 16
    return pl.pallas_call(
        functools.partial(first_kernel, owner, block, chunk),
        in_specs=[SMEM] * 4 + [VMEM] * 7,
        out_specs=VMEM,
        out_shape=jax.ShapeDtypeStruct((2, block, cols), jnp.bfloat16),
        scratch_shapes=[
            pltpu.VMEM((2 * rows, 2 * cols), jnp.bfloat16),
            pltpu.VMEM((span, cols), jnp.float32),
            pltpu.VMEM((span, cols), jnp.float32),
            pltpu.VMEM((span, HD), jnp.float32),
        ],
        compiler_params=pltpu.CompilerParams(vmem_limit_bytes=28 * MIB),
        cost_estimate=pl.CostEstimate(
            flops=4 * span * width * cols, bytes_accessed=2 * (span * width + 2 * width * cols), transcendentals=0
        ),
        name="first_block",
    )(*places, peer, wk, wv, gain, cosine, sine, own)


def peer_kernel(
    far, block, chunk, offset_ref, length_ref, owner_ref, slot_ref,
    h_ref, wk_ref, wv_ref, gain_ref, cos_ref, sin_ref, own_ref, factor_ref, kv_ref, *rest
):
    blocks, (acc_k, acc_v) = rest[: len(far)], rest[len(far) :]
    rows, width = h_ref.shape
    cols = acc_k.shape[1]
    mine = lax.axis_index("tensor")
    there = pl.ds(pl.multiple_of((1 - mine) * rows, rows), rows)
    here = pl.ds(pl.multiple_of(mine * rows, rows), rows)
    project(h_ref, slice(None), gain_ref, wk_ref, wv_ref, acc_k, acc_v, factor_ref[:, :1], chunk)
    keys, values = finish(cos_ref[there, :], sin_ref[there, :], acc_k, acc_v)
    kv_ref[there, :cols] = keys
    kv_ref[there, cols:] = values
    kv_ref[here, :] = own_ref[...]
    places = (offset_ref, length_ref, owner_ref, slot_ref)
    for k, out_ref in zip(far, blocks):
        select_block(block, cols, jnp.bitwise_xor(lax.axis_index("dp"), k), places, kv_ref, out_ref)


def peer_rows(far, block, places, peer, wk, wv, gain, cosine, sine, own, factor, chunk=1024):
    rows, width = peer.shape
    cols = wk.shape[1]
    tok_rows = cosine.shape[0]
    return pl.pallas_call(
        functools.partial(peer_kernel, far, block, chunk),
        in_specs=[SMEM] * 4 + [VMEM] * 8,
        out_specs=[VMEM] * (1 + len(far)),
        out_shape=[jax.ShapeDtypeStruct((tok_rows, 2 * cols), jnp.bfloat16)]
        + [jax.ShapeDtypeStruct((2, block, cols), jnp.bfloat16)] * len(far),
        scratch_shapes=[
            pltpu.VMEM((rows, cols), jnp.float32),
            pltpu.VMEM((rows, cols), jnp.float32),
        ],
        compiler_params=pltpu.CompilerParams(vmem_limit_bytes=28 * MIB),
        cost_estimate=pl.CostEstimate(
            flops=4 * rows * width * cols, bytes_accessed=2 * (rows * width + 2 * width * cols), transcendentals=0
        ),
        name="peer_rows",
    )(*places, peer, wk, wv, gain, cosine, sine, own, factor)


def attend_kernel(tile, window, offset_ref, q_ref, kv_ref, out_ref):
    cols = kv_ref.shape[1] // 2
    groups = cols // HD
    heads = q_ref.shape[1] // HD // groups
    first = pl.program_id(0) * tile
    start = pl.multiple_of(jnp.maximum(first + tile - window, 0), 16)
    row = first + lax.broadcasted_iota(jnp.int32, (tile, window), 0)
    key = start + lax.broadcasted_iota(jnp.int32, (tile, window), 1)
    allowed = (key <= row) & (key >= prompt_start(row, offset_ref))
    bias = jnp.where(allowed, 0.0, -1e30)[None]
    ones = jnp.ones((window, HD), jnp.bfloat16)
    scale = HD**-0.5 * float(np.log2(np.e))
    for g in range(groups):
        at = [slice((g * heads + h) * HD, (g * heads + h + 1) * HD) for h in range(heads)]
        q = jnp.concatenate([q_ref[:, a] for a in at], axis=0)
        k = kv_ref[pl.ds(start, window), g * HD : (g + 1) * HD]
        v = kv_ref[pl.ds(start, window), cols + g * HD : cols + (g + 1) * HD]
        scores = lax.dot_general(q, k, (((1,), (1,)), ((), ())), preferred_element_type=jnp.float32)
        scores = scores.reshape(heads, tile, window) * scale + bias
        exponent = jnp.exp2(scores - jnp.max(scores, axis=2, keepdims=True))
        exponent = exponent.astype(jnp.bfloat16).reshape(heads * tile, window)
        summed = jnp.dot(exponent, jnp.concatenate([v, ones], axis=1), preferred_element_type=jnp.float32)
        result = (summed[:, :HD] / summed[:, HD:]).astype(jnp.bfloat16)
        for h, a in enumerate(at):
            out_ref[:, a] = result[h * tile : (h + 1) * tile]


def attend(offsets, queries, kv, longest, tile=64):
    rows, width = queries.shape
    window = tile + longest
    rows_at = pl.BlockSpec((tile, width), lambda i: (i, 0))
    return pl.pallas_call(
        functools.partial(attend_kernel, tile, window),
        grid=(rows // tile,),
        in_specs=[SMEM, rows_at, pl.BlockSpec(kv.shape, lambda i: (0, 0))],
        out_specs=rows_at,
        out_shape=jax.ShapeDtypeStruct((rows, width), jnp.bfloat16),
        compiler_params=pltpu.CompilerParams(vmem_limit_bytes=32 * MIB),
        cost_estimate=pl.CostEstimate(
            flops=4 * rows * width * window,
            bytes_accessed=4 * rows * width,
            transcendentals=rows * window * width // HD,
        ),
        name="attend",
    )(offsets, queries, kv)


def gather_kernel(order, block, *refs):
    key_ref, value_ref, sems = refs[-3:]
    me = lax.axis_index("dp")
    copies = []
    for i, k in enumerate(order):
        rows = pl.ds(pl.multiple_of(jnp.bitwise_xor(me, k) * block, block), block)
        for n, out_ref in enumerate((key_ref, value_ref)):
            copies.append(pltpu.make_async_copy(refs[i].at[n], out_ref.at[rows, :], sems.at[i, n]))
    for copy in copies:
        copy.start()
    for copy in copies:
        copy.wait()


def place(order, block, blocks, cache, before=()):
    n = len(order)
    anywhere = pl.BlockSpec(memory_space=pl.ANY)
    return pl.pallas_call(
        functools.partial(gather_kernel, order, block),
        in_specs=[VMEM] * n + [anywhere] * len(before),
        out_specs=[anywhere] * 2,
        out_shape=[cache, cache],
        input_output_aliases={n: 0, n + 1: 1} if before else {},
        scratch_shapes=[pltpu.SemaphoreType.DMA((n, 2))],
        compiler_params=pltpu.CompilerParams(vmem_limit_bytes=8 * MIB),
        name="place_rest" if before else "place_first",
    )(*blocks, *before)


def on_device(
    hidden, norm_gain, key_weight, value_weight, queries,
    segment_ids, prompt_lengths, prompt_offsets, decode_owner, slot_offsets,
):
    n_dp = lax.axis_size("dp")
    half, width = hidden.shape
    tok_rows = queries.shape[0]
    cols = key_weight.shape[1]
    block = 2 * tok_rows // n_dp
    gain = norm_gain.reshape(1, width)

    peer = lax.ppermute(hidden, "tensor", [(0, 1), (1, 0)])
    own, factor, cosine, sine, wk, wv = own_rows(
        block, prompt_offsets, hidden, key_weight, value_weight, gain, tok_rows
    )
    places = [prompt_offsets, prompt_lengths, decode_owner, slot_offsets]
    swap = lambda a, k: lax.ppermute(a, "dp", [(p, p ^ k) for p in range(n_dp)]) if k else a
    half_dp = n_dp // 2
    far = list(range(half_dp, n_dp))
    near = list(range(1, half_dp))
    order = (far[2], far[1], *near[1:], far[0], *far[3:], near[0], 0)
    factor = lax.ppermute(factor, "tensor", [(0, 1), (1, 0)])
    first = first_block(order[0], block, places, peer, wk, wv, gain, cosine, sine, own)
    kv, *blocks = peer_rows(order[1:], block, places, peer, wk, wv, gain, cosine, sine, own, factor)
    first = swap(first, order[0])
    first, *blocks[4:-1] = lax.optimization_barrier((first, *blocks[4:-1]))
    received = [first] + [swap(a, k) for k, a in zip(order[1:], blocks)]
    attended = attend(prompt_offsets, queries, kv, block)
    cache = jax.ShapeDtypeStruct((n_dp * block, cols), jnp.bfloat16)
    by_place = dict(zip(order, received))
    early = (0, *order[: n_dp // 2 + 1])
    late = tuple(k for k in order if k not in early)
    caches = place(early, block, [by_place[k] for k in early], cache)
    key_cache, value_cache = place(late, block, [by_place[k] for k in late], cache, caches)
    return attended, key_cache[None], value_cache[None]


def solution(mesh):
    rows = P(("groups", "dp"))
    in_specs = (
        P(("groups", "dp", "tensor"), None),
        P(),
        P(None, "tensor"),
        P(None, "tensor"),
        P(("groups", "dp"), "tensor"),
        rows, rows, rows, rows, rows,
    )
    out_specs = (
        P(("groups", "dp"), "tensor"),
        P(("groups", "dp"), None, "tensor"),
        P(("groups", "dp"), None, "tensor"),
    )
    return jax.shard_map(on_device, mesh=mesh, in_specs=in_specs, out_specs=out_specs, check_vma=False)
```

```python
import functools

import jax
import jax.numpy as jnp
import numpy as np
from jax import lax
from jax.experimental import pallas as pl
from jax.experimental.pallas import tpu as pltpu
from jax.sharding import PartitionSpec as P

HD = 128
EPSILON = 1e-05
ROPE_BASE = 500000.0
MIB = 1024 * 1024
SMEM = pl.BlockSpec(memory_space=pltpu.SMEM)
VMEM = pl.BlockSpec(memory_space=pltpu.VMEM)


def prompt_start(rows, offset_ref):
    start = jnp.zeros_like(rows)
    for s in range(offset_ref.shape[1]):
        offset = offset_ref[0, s]
        start = jnp.where(rows >= offset, jnp.maximum(start, offset), start)
    return start


def rotation_tables(block, offset_ref, cos_ref, sin_ref):
    position = lax.broadcasted_iota(jnp.int32, (block, HD), 0).astype(jnp.float32)
    lane = lax.broadcasted_iota(jnp.int32, (block, HD), 1)
    half = lax.broadcasted_iota(jnp.int32, (1, HD), 1) % (HD // 2)
    inverse = jnp.zeros((1, HD), jnp.float32)
    for i in range(HD // 2):
        inverse = jnp.where(half == i, np.float32(ROPE_BASE ** (-2.0 * i / HD)), inverse)
    angle = position * inverse
    cosine = jnp.cos(angle)
    sine = jnp.where(lane < HD // 2, -1.0, 1.0) * jnp.sin(angle)
    for s in range(offset_ref.shape[1]):
        rows = pl.ds(offset_ref[0, s], block)
        cos_ref[rows, :] = cosine
        sin_ref[rows, :] = sine


def norm_factor(h_ref, rows, squares, chunk, ready=None):
    width = h_ref.shape[1]
    for c in range(width // chunk):
        if ready is not None:
            ready(c)
        h = h_ref[rows, c * chunk : (c + 1) * chunk]
        parts = [h[:, j * HD : (j + 1) * HD].astype(jnp.float32) for j in range(chunk // HD)]
        total = sum(p * p for p in parts)
        squares[...] = total if c == 0 else squares[...] + total
    return lax.rsqrt(jnp.sum(squares[...], axis=1, keepdims=True) / width + EPSILON)


def project(h_ref, rows, gain_ref, wk_ref, wv_ref, acc_k, acc_v, factor, chunk, loaded=None):
    width = h_ref.shape[1]
    for c in range(width // chunk):
        if loaded is not None:
            loaded(c)
        at = slice(c * chunk, (c + 1) * chunk)
        normed = h_ref[rows, at].astype(jnp.float32) * factor * gain_ref[:, at].astype(jnp.float32)
        normed = normed.astype(jnp.bfloat16)
        for w_ref, acc in ((wk_ref, acc_k), (wv_ref, acc_v)):
            product = jnp.dot(normed, w_ref[at, :], preferred_element_type=jnp.float32)
            acc[...] = product if c == 0 else acc[...] + product


def finish(cosine, sine, acc_k, acc_v):
    keys = []
    for h in range(acc_k.shape[1] // HD):
        x = acc_k[:, h * HD : (h + 1) * HD]
        keys.append((x * cosine + pltpu.roll(x, HD // 2, 1) * sine).astype(jnp.bfloat16))
    return jnp.concatenate(keys, axis=1), acc_v[...].astype(jnp.bfloat16)


def own_kernel(
    chunk, h_hbm, wk_hbm, wv_hbm, gain_ref,
    key_ref, value_ref, factor_ref, wk_ref, wv_ref, h_ref, acc_k, acc_v, squares, sems
):
    rows, width = h_hbm.shape
    cols = acc_k.shape[1]

    def copies(c):
        at = pl.ds(c * chunk, chunk)
        return (
            pltpu.make_async_copy(h_hbm.at[:, at], h_ref.at[:, at], sems.at[c, 0]),
            pltpu.make_async_copy(wk_hbm.at[at, :], wk_ref.at[at, :], sems.at[c, 1]),
            pltpu.make_async_copy(wv_hbm.at[at, :], wv_ref.at[at, :], sems.at[c, 2]),
        )

    def ready(c):
        copies(c)[0].wait()

    def loaded(c):
        for copy in copies(c)[1:]:
            copy.wait()

    for c in range(width // chunk):
        copies(c)[0].start()
    for c in range(width // chunk):
        for copy in copies(c)[1:]:
            copy.start()
    factor = norm_factor(h_ref, slice(None), squares, chunk, ready)
    factor_ref[...] = jnp.broadcast_to(factor, factor_ref.shape)
    project(h_ref, slice(None), gain_ref, wk_ref, wv_ref, acc_k, acc_v, factor, chunk, loaded)
    key_ref[...] = acc_k[...]
    value_ref[...] = acc_v[...].astype(jnp.bfloat16)


def rotate_kernel(block, offset_ref, key_ref, value_ref, out_ref, cos_ref, sin_ref, cos_pad, sin_pad):
    rows, cols = key_ref.shape
    rotation_tables(block, offset_ref, cos_pad, sin_pad)
    cos_ref[...] = cos_pad[: cos_ref.shape[0], :]
    sin_ref[...] = sin_pad[: sin_ref.shape[0], :]
    here = pl.ds(pl.multiple_of(lax.axis_index("tensor") * rows, rows), rows)
    keys, values = finish(cos_pad[here, :], sin_pad[here, :], key_ref, value_ref)
    out_ref[:, :cols] = keys
    out_ref[:, cols:] = values


def rotate_own(block, offsets, keys, values):
    rows, cols = keys.shape
    table = jax.ShapeDtypeStruct((2 * rows, HD), jnp.float32)
    pad = pltpu.VMEM((2 * rows + block, HD), jnp.float32)
    return pl.pallas_call(
        functools.partial(rotate_kernel, block),
        in_specs=[SMEM, VMEM, VMEM],
        out_specs=[VMEM] * 3,
        out_shape=[jax.ShapeDtypeStruct((rows, 2 * cols), jnp.bfloat16), table, table],
        scratch_shapes=[pad, pad],
        compiler_params=pltpu.CompilerParams(vmem_limit_bytes=28 * MIB),
        name="rotate_own",
    )(offsets, keys, values)


def own_rows(hidden, wk, wv, gain, chunk=1024):
    rows, width = hidden.shape
    cols = wk.shape[1]
    hbm = pl.BlockSpec(memory_space=pltpu.HBM)
    f32 = jnp.float32
    return pl.pallas_call(
        functools.partial(own_kernel, chunk),
        in_specs=[hbm, hbm, hbm, VMEM],
        out_specs=[VMEM] * 5,
        out_shape=[
            jax.ShapeDtypeStruct((rows, cols), f32),
            jax.ShapeDtypeStruct((rows, cols), jnp.bfloat16),
            jax.ShapeDtypeStruct((rows, HD), f32),
            jax.ShapeDtypeStruct(wk.shape, wk.dtype),
            jax.ShapeDtypeStruct(wv.shape, wv.dtype),
        ],
        scratch_shapes=[
            pltpu.VMEM((rows, width), jnp.bfloat16),
            pltpu.VMEM((rows, cols), f32),
            pltpu.VMEM((rows, cols), f32),
            pltpu.VMEM((rows, HD), f32),
            pltpu.SemaphoreType.DMA((width // chunk, 3)),
        ],
        compiler_params=pltpu.CompilerParams(vmem_limit_bytes=45 * MIB),
        cost_estimate=pl.CostEstimate(
            flops=4 * rows * width * cols, bytes_accessed=2 * (rows * width + 2 * width * cols), transcendentals=0
        ),
        name="own_rows",
    )(hidden, wk, wv, gain)


def select_block(block, cols, owner, places, kv_ref, out_ref):
    offset_ref, length_ref, owner_ref, slot_ref = places
    offset = jnp.int32(0)
    length = jnp.int32(0)
    slot = jnp.int32(0)
    for s in range(owner_ref.shape[1]):
        hit = owner_ref[0, s] == owner
        offset = jnp.where(hit, offset_ref[0, s], offset)
        length = jnp.where(hit, length_ref[0, s], length)
        slot = jnp.where(hit, slot_ref[0, s], slot)
    span = block + 16
    start = jnp.minimum((offset // 16) * 16, kv_ref.shape[0] - span)
    start = pl.multiple_of(start, 16)
    place = lax.broadcasted_iota(jnp.int32, (block, span), 0) + (lax.axis_index("dp") * block - slot)
    token = lax.broadcasted_iota(jnp.int32, (block, span), 1) + (start - offset)
    chosen = (place == token) & (place >= 0) & (place < length)
    picked = jnp.dot(
        jnp.where(chosen, 1.0, 0.0).astype(jnp.bfloat16),
        kv_ref[pl.ds(start, span), :],
        preferred_element_type=jnp.float32,
    ).astype(jnp.bfloat16)
    out_ref[0] = picked[:, :cols]
    out_ref[1] = picked[:, cols:]


def first_kernel(
    owner, block, chunk, offset_ref, length_ref, owner_ref, slot_ref,
    h_ref, wk_ref, wv_ref, gain_ref, cos_ref, sin_ref, own_ref, factor_ref, block_ref, kv, acc_k, acc_v
):
    rows, width = h_ref.shape
    cols = acc_k.shape[1]
    span = acc_k.shape[0]
    mine = lax.axis_index("tensor")
    owner = jnp.bitwise_xor(lax.axis_index("dp"), owner)
    here = pl.ds(pl.multiple_of(mine * rows, rows), rows)
    kv[here, :] = own_ref[...]
    offset = jnp.int32(0)
    for s in range(owner_ref.shape[1]):
        offset = jnp.where(owner_ref[0, s] == owner, offset_ref[0, s], offset)
    start = jnp.minimum((offset // 16) * 16, 2 * rows - span)
    local = pl.multiple_of(jnp.clip(start - (1 - mine) * rows, 0, rows - span), 16)
    there = pl.ds(pl.multiple_of((1 - mine) * rows + local, 16), span)
    factor = factor_ref[pl.ds(local, span), :1]
    project(h_ref, pl.ds(local, span), gain_ref, wk_ref, wv_ref, acc_k, acc_v, factor, chunk)
    keys, values = finish(cos_ref[there, :], sin_ref[there, :], acc_k, acc_v)
    kv[there, :cols] = keys
    kv[there, cols:] = values
    select_block(block, cols, owner, (offset_ref, length_ref, owner_ref, slot_ref), kv, block_ref)


def first_block(owner, block, places, peer, wk, wv, gain, cosine, sine, own, factor, chunk=1024):
    rows, width = peer.shape
    cols = wk.shape[1]
    span = block + 16
    return pl.pallas_call(
        functools.partial(first_kernel, owner, block, chunk),
        in_specs=[SMEM] * 4 + [VMEM] * 8,
        out_specs=VMEM,
        out_shape=jax.ShapeDtypeStruct((2, block, cols), jnp.bfloat16),
        scratch_shapes=[
            pltpu.VMEM((2 * rows, 2 * cols), jnp.bfloat16),
            pltpu.VMEM((span, cols), jnp.float32),
            pltpu.VMEM((span, cols), jnp.float32),
        ],
        compiler_params=pltpu.CompilerParams(vmem_limit_bytes=28 * MIB),
        cost_estimate=pl.CostEstimate(
            flops=4 * span * width * cols, bytes_accessed=2 * (span * width + 2 * width * cols), transcendentals=0
        ),
        name="first_block",
    )(*places, peer, wk, wv, gain, cosine, sine, own, factor)


def peer_kernel(
    far, block, chunk, offset_ref, length_ref, owner_ref, slot_ref,
    h_ref, wk_ref, wv_ref, gain_ref, cos_ref, sin_ref, own_ref, factor_ref, kv_ref, *rest
):
    blocks, (acc_k, acc_v) = rest[: len(far)], rest[len(far) :]
    rows, width = h_ref.shape
    cols = acc_k.shape[1]
    mine = lax.axis_index("tensor")
    there = pl.ds(pl.multiple_of((1 - mine) * rows, rows), rows)
    here = pl.ds(pl.multiple_of(mine * rows, rows), rows)
    project(h_ref, slice(None), gain_ref, wk_ref, wv_ref, acc_k, acc_v, factor_ref[:, :1], chunk)
    keys, values = finish(cos_ref[there, :], sin_ref[there, :], acc_k, acc_v)
    kv_ref[there, :cols] = keys
    kv_ref[there, cols:] = values
    kv_ref[here, :] = own_ref[...]
    places = (offset_ref, length_ref, owner_ref, slot_ref)
    for k, out_ref in zip(far, blocks):
        select_block(block, cols, jnp.bitwise_xor(lax.axis_index("dp"), k), places, kv_ref, out_ref)


def peer_rows(far, block, places, peer, wk, wv, gain, cosine, sine, own, factor, chunk=1024):
    rows, width = peer.shape
    cols = wk.shape[1]
    tok_rows = cosine.shape[0]
    return pl.pallas_call(
        functools.partial(peer_kernel, far, block, chunk),
        in_specs=[SMEM] * 4 + [VMEM] * 8,
        out_specs=[VMEM] * (1 + len(far)),
        out_shape=[jax.ShapeDtypeStruct((tok_rows, 2 * cols), jnp.bfloat16)]
        + [jax.ShapeDtypeStruct((2, block, cols), jnp.bfloat16)] * len(far),
        scratch_shapes=[
            pltpu.VMEM((rows, cols), jnp.float32),
            pltpu.VMEM((rows, cols), jnp.float32),
        ],
        compiler_params=pltpu.CompilerParams(vmem_limit_bytes=28 * MIB),
        cost_estimate=pl.CostEstimate(
            flops=4 * rows * width * cols, bytes_accessed=2 * (rows * width + 2 * width * cols), transcendentals=0
        ),
        name="peer_rows",
    )(*places, peer, wk, wv, gain, cosine, sine, own, factor)


def attend_kernel(tile, window, offset_ref, q_ref, kv_ref, out_ref):
    cols = kv_ref.shape[1] // 2
    groups = cols // HD
    heads = q_ref.shape[1] // HD // groups
    first = pl.program_id(0) * tile
    start = pl.multiple_of(jnp.maximum(first + tile - window, 0), 16)
    row = first + lax.broadcasted_iota(jnp.int32, (tile, window), 0)
    key = start + lax.broadcasted_iota(jnp.int32, (tile, window), 1)
    allowed = (key <= row) & (key >= prompt_start(row, offset_ref))
    bias = jnp.where(allowed, 0.0, -1e30)[None]
    ones = jnp.ones((window, HD), jnp.bfloat16)
    scale = HD**-0.5 * float(np.log2(np.e))
    for g in range(groups):
        at = [slice((g * heads + h) * HD, (g * heads + h + 1) * HD) for h in range(heads)]
        q = jnp.concatenate([q_ref[:, a] for a in at], axis=0)
        k = kv_ref[pl.ds(start, window), g * HD : (g + 1) * HD]
        v = kv_ref[pl.ds(start, window), cols + g * HD : cols + (g + 1) * HD]
        scores = lax.dot_general(q, k, (((1,), (1,)), ((), ())), preferred_element_type=jnp.float32)
        scores = scores.reshape(heads, tile, window) * scale + bias
        exponent = jnp.exp2(scores - jnp.max(scores, axis=2, keepdims=True))
        exponent = exponent.astype(jnp.bfloat16).reshape(heads * tile, window)
        summed = jnp.dot(exponent, jnp.concatenate([v, ones], axis=1), preferred_element_type=jnp.float32)
        result = (summed[:, :HD] / summed[:, HD:]).astype(jnp.bfloat16)
        for h, a in enumerate(at):
            out_ref[:, a] = result[h * tile : (h + 1) * tile]


def attend(offsets, queries, kv, longest, tile=64):
    rows, width = queries.shape
    window = tile + longest
    rows_at = pl.BlockSpec((tile, width), lambda i: (i, 0))
    return pl.pallas_call(
        functools.partial(attend_kernel, tile, window),
        grid=(rows // tile,),
        in_specs=[SMEM, rows_at, pl.BlockSpec(kv.shape, lambda i: (0, 0))],
        out_specs=rows_at,
        out_shape=jax.ShapeDtypeStruct((rows, width), jnp.bfloat16),
        compiler_params=pltpu.CompilerParams(vmem_limit_bytes=32 * MIB),
        cost_estimate=pl.CostEstimate(
            flops=4 * rows * width * window,
            bytes_accessed=4 * rows * width,
            transcendentals=rows * window * width // HD,
        ),
        name="attend",
    )(offsets, queries, kv)


def gather_kernel(order, block, *refs):
    key_ref, value_ref, sems = refs[-3:]
    me = lax.axis_index("dp")
    copies = []
    for i, k in enumerate(order):
        rows = pl.ds(pl.multiple_of(jnp.bitwise_xor(me, k) * block, block), block)
        for n, out_ref in enumerate((key_ref, value_ref)):
            copies.append(pltpu.make_async_copy(refs[i].at[n], out_ref.at[rows, :], sems.at[i, n]))
    for copy in copies:
        copy.start()
    for copy in copies:
        copy.wait()


def place(order, block, blocks, cache, before=()):
    n = len(order)
    anywhere = pl.BlockSpec(memory_space=pl.ANY)
    return pl.pallas_call(
        functools.partial(gather_kernel, order, block),
        in_specs=[VMEM] * n + [anywhere] * len(before),
        out_specs=[anywhere] * 2,
        out_shape=[cache, cache],
        input_output_aliases={n: 0, n + 1: 1} if before else {},
        scratch_shapes=[pltpu.SemaphoreType.DMA((n, 2))],
        compiler_params=pltpu.CompilerParams(vmem_limit_bytes=8 * MIB),
        name="place_rest" if before else "place_first",
    )(*blocks, *before)


def on_device(
    hidden, norm_gain, key_weight, value_weight, queries,
    segment_ids, prompt_lengths, prompt_offsets, decode_owner, slot_offsets,
):
    n_dp = lax.axis_size("dp")
    half, width = hidden.shape
    tok_rows = queries.shape[0]
    cols = key_weight.shape[1]
    block = 2 * tok_rows // n_dp
    gain = norm_gain.reshape(1, width)

    peer = lax.ppermute(hidden, "tensor", [(0, 1), (1, 0)])
    own_k, own_v, factor, wk, wv = own_rows(hidden, key_weight, value_weight, gain)
    own, cosine, sine = rotate_own(block, prompt_offsets, own_k, own_v)
    places = [prompt_offsets, prompt_lengths, decode_owner, slot_offsets]
    swap = lambda a, k: lax.ppermute(a, "dp", [(p, p ^ k) for p in range(n_dp)]) if k else a
    half_dp = n_dp // 2
    far = list(range(half_dp, n_dp))
    near = list(range(1, half_dp))
    order = (far[2], far[1], *near[1:], far[0], *far[3:], near[0], 0)
    factor = lax.ppermute(factor, "tensor", [(0, 1), (1, 0)])
    first = first_block(order[0], block, places, peer, wk, wv, gain, cosine, sine, own, factor)
    kv, *blocks = peer_rows(order[1:], block, places, peer, wk, wv, gain, cosine, sine, own, factor)
    first = swap(first, order[0])
    first, *blocks[4:-1] = lax.optimization_barrier((first, *blocks[4:-1]))
    received = [first] + [swap(a, k) for k, a in zip(order[1:], blocks)]
    attended = attend(prompt_offsets, queries, kv, block)
    cache = jax.ShapeDtypeStruct((n_dp * block, cols), jnp.bfloat16)
    by_place = dict(zip(order, received))
    early = (0, *order[: n_dp // 2 + 1])
    late = tuple(k for k in order if k not in early)
    caches = place(early, block, [by_place[k] for k in early], cache)
    key_cache, value_cache = place(late, block, [by_place[k] for k in late], cache, caches)
    return attended, key_cache[None], value_cache[None]


def solution(mesh):
    rows = P(("groups", "dp"))
    in_specs = (
        P(("groups", "dp", "tensor"), None),
        P(),
        P(None, "tensor"),
        P(None, "tensor"),
        P(("groups", "dp"), "tensor"),
        rows, rows, rows, rows, rows,
    )
    out_specs = (
        P(("groups", "dp"), "tensor"),
        P(("groups", "dp"), None, "tensor"),
        P(("groups", "dp"), None, "tensor"),
    )
    return jax.shard_map(on_device, mesh=mesh, in_specs=in_specs, out_specs=out_specs, check_vma=False)
```

```python
import functools

import jax
import jax.numpy as jnp
import numpy as np
from jax import lax
from jax.experimental import pallas as pl
from jax.experimental.pallas import tpu as pltpu
from jax.sharding import PartitionSpec as P

HD = 128
EPSILON = 1e-05
ROPE_BASE = 500000.0
MIB = 1024 * 1024
SMEM = pl.BlockSpec(memory_space=pltpu.SMEM)
VMEM = pl.BlockSpec(memory_space=pltpu.VMEM)


def prompt_start(rows, offset_ref):
    start = jnp.zeros_like(rows)
    for s in range(offset_ref.shape[1]):
        offset = offset_ref[0, s]
        start = jnp.where(rows >= offset, jnp.maximum(start, offset), start)
    return start


def rotation_tables(block, offset_ref, cos_ref, sin_ref):
    position = lax.broadcasted_iota(jnp.int32, (block, HD), 0).astype(jnp.float32)
    lane = lax.broadcasted_iota(jnp.int32, (block, HD), 1)
    half = lax.broadcasted_iota(jnp.int32, (1, HD), 1) % (HD // 2)
    inverse = jnp.zeros((1, HD), jnp.float32)
    for i in range(HD // 2):
        inverse = jnp.where(half == i, np.float32(ROPE_BASE ** (-2.0 * i / HD)), inverse)
    angle = position * inverse
    cosine = jnp.cos(angle)
    sine = jnp.where(lane < HD // 2, -1.0, 1.0) * jnp.sin(angle)
    for s in range(offset_ref.shape[1]):
        rows = pl.ds(offset_ref[0, s], block)
        cos_ref[rows, :] = cosine
        sin_ref[rows, :] = sine


def norm_factor(h_ref, rows, squares, chunk, ready=None):
    width = h_ref.shape[1]
    for c in range(width // chunk):
        if ready is not None:
            ready(c)
        h = h_ref[rows, c * chunk : (c + 1) * chunk]
        parts = [h[:, j * HD : (j + 1) * HD].astype(jnp.float32) for j in range(chunk // HD)]
        total = sum(p * p for p in parts)
        squares[...] = total if c == 0 else squares[...] + total
    return lax.rsqrt(jnp.sum(squares[...], axis=1, keepdims=True) / width + EPSILON)


def project(h_ref, rows, gain_ref, wk_ref, wv_ref, acc_k, acc_v, factor, chunk, loaded=None):
    width = h_ref.shape[1]
    for c in range(width // chunk):
        if loaded is not None:
            loaded(c)
        at = slice(c * chunk, (c + 1) * chunk)
        normed = h_ref[rows, at].astype(jnp.float32) * factor * gain_ref[:, at].astype(jnp.float32)
        normed = normed.astype(jnp.bfloat16)
        for w_ref, acc in ((wk_ref, acc_k), (wv_ref, acc_v)):
            product = jnp.dot(normed, w_ref[at, :], preferred_element_type=jnp.float32)
            acc[...] = product if c == 0 else acc[...] + product


def finish(cosine, sine, acc_k, acc_v):
    keys = []
    for h in range(acc_k.shape[1] // HD):
        x = acc_k[:, h * HD : (h + 1) * HD]
        keys.append((x * cosine + pltpu.roll(x, HD // 2, 1) * sine).astype(jnp.bfloat16))
    return jnp.concatenate(keys, axis=1), acc_v[...].astype(jnp.bfloat16)


def own_kernel(
    chunk, h_hbm, wk_hbm, wv_hbm, gain_ref,
    key_ref, value_ref, factor_ref, wk_ref, wv_ref, h_ref, acc_k, acc_v, squares, sems
):
    rows, width = h_hbm.shape
    cols = acc_k.shape[1]

    def copies(c):
        at = pl.ds(c * chunk, chunk)
        return (
            pltpu.make_async_copy(h_hbm.at[:, at], h_ref.at[:, at], sems.at[c, 0]),
            pltpu.make_async_copy(wk_hbm.at[at, :], wk_ref.at[at, :], sems.at[c, 1]),
            pltpu.make_async_copy(wv_hbm.at[at, :], wv_ref.at[at, :], sems.at[c, 2]),
        )

    def ready(c):
        copies(c)[0].wait()

    def loaded(c):
        for copy in copies(c)[1:]:
            copy.wait()

    for c in range(width // chunk):
        copies(c)[0].start()
    for c in range(width // chunk):
        for copy in copies(c)[1:]:
            copy.start()
    factor = norm_factor(h_ref, slice(None), squares, chunk, ready)
    factor_ref[...] = jnp.broadcast_to(factor, factor_ref.shape)
    project(h_ref, slice(None), gain_ref, wk_ref, wv_ref, acc_k, acc_v, factor, chunk, loaded)
    key_ref[...] = acc_k[...]
    value_ref[...] = acc_v[...].astype(jnp.bfloat16)


def rotate_kernel(block, offset_ref, key_ref, value_ref, out_ref, cos_ref, sin_ref, cos_pad, sin_pad):
    rows, cols = key_ref.shape
    rotation_tables(block, offset_ref, cos_pad, sin_pad)
    cos_ref[...] = cos_pad[: cos_ref.shape[0], :]
    sin_ref[...] = sin_pad[: sin_ref.shape[0], :]
    here = pl.ds(pl.multiple_of(lax.axis_index("tensor") * rows, rows), rows)
    keys, values = finish(cos_pad[here, :], sin_pad[here, :], key_ref, value_ref)
    out_ref[:, :cols] = keys
    out_ref[:, cols:] = values


def rotate_own(block, offsets, keys, values):
    rows, cols = keys.shape
    table = jax.ShapeDtypeStruct((2 * rows, HD), jnp.float32)
    pad = pltpu.VMEM((2 * rows + block, HD), jnp.float32)
    return pl.pallas_call(
        functools.partial(rotate_kernel, block),
        in_specs=[SMEM, VMEM, VMEM],
        out_specs=[VMEM] * 3,
        out_shape=[jax.ShapeDtypeStruct((rows, 2 * cols), jnp.bfloat16), table, table],
        scratch_shapes=[pad, pad],
        compiler_params=pltpu.CompilerParams(vmem_limit_bytes=28 * MIB),
        name="rotate_own",
    )(offsets, keys, values)


def own_rows(hidden, wk, wv, gain, chunk=1024):
    rows, width = hidden.shape
    cols = wk.shape[1]
    hbm = pl.BlockSpec(memory_space=pltpu.HBM)
    f32 = jnp.float32
    return pl.pallas_call(
        functools.partial(own_kernel, chunk),
        in_specs=[hbm, hbm, hbm, VMEM],
        out_specs=[VMEM] * 5,
        out_shape=[
            jax.ShapeDtypeStruct((rows, cols), f32),
            jax.ShapeDtypeStruct((rows, cols), jnp.bfloat16),
            jax.ShapeDtypeStruct((rows, HD), f32),
            jax.ShapeDtypeStruct(wk.shape, wk.dtype),
            jax.ShapeDtypeStruct(wv.shape, wv.dtype),
        ],
        scratch_shapes=[
            pltpu.VMEM((rows, width), jnp.bfloat16),
            pltpu.VMEM((rows, cols), f32),
            pltpu.VMEM((rows, cols), f32),
            pltpu.VMEM((rows, HD), f32),
            pltpu.SemaphoreType.DMA((width // chunk, 3)),
        ],
        compiler_params=pltpu.CompilerParams(vmem_limit_bytes=45 * MIB),
        cost_estimate=pl.CostEstimate(
            flops=4 * rows * width * cols, bytes_accessed=2 * (rows * width + 2 * width * cols), transcendentals=0
        ),
        name="own_rows",
    )(hidden, wk, wv, gain)


def select_block(block, cols, owner, places, kv_ref, out_ref):
    offset_ref, length_ref, owner_ref, slot_ref = places
    offset = jnp.int32(0)
    length = jnp.int32(0)
    slot = jnp.int32(0)
    for s in range(owner_ref.shape[1]):
        hit = owner_ref[0, s] == owner
        offset = jnp.where(hit, offset_ref[0, s], offset)
        length = jnp.where(hit, length_ref[0, s], length)
        slot = jnp.where(hit, slot_ref[0, s], slot)
    span = block + 16
    start = jnp.minimum((offset // 16) * 16, kv_ref.shape[0] - span)
    start = pl.multiple_of(start, 16)
    place = lax.broadcasted_iota(jnp.int32, (block, span), 0) + (lax.axis_index("dp") * block - slot)
    token = lax.broadcasted_iota(jnp.int32, (block, span), 1) + (start - offset)
    chosen = (place == token) & (place >= 0) & (place < length)
    picked = jnp.dot(
        jnp.where(chosen, 1.0, 0.0).astype(jnp.bfloat16),
        kv_ref[pl.ds(start, span), :],
        preferred_element_type=jnp.float32,
    ).astype(jnp.bfloat16)
    out_ref[0] = picked[:, :cols]
    out_ref[1] = picked[:, cols:]


def first_kernel(
    owner, block, chunk, offset_ref, length_ref, owner_ref, slot_ref,
    h_ref, wk_ref, wv_ref, gain_ref, cos_ref, sin_ref, own_ref, factor_ref, block_ref, kv, acc_k, acc_v
):
    rows, width = h_ref.shape
    cols = acc_k.shape[1]
    span = acc_k.shape[0]
    mine = lax.axis_index("tensor")
    owner = jnp.bitwise_xor(lax.axis_index("dp"), owner)
    here = pl.ds(pl.multiple_of(mine * rows, rows), rows)
    kv[here, :] = own_ref[...]
    offset = jnp.int32(0)
    for s in range(owner_ref.shape[1]):
        offset = jnp.where(owner_ref[0, s] == owner, offset_ref[0, s], offset)
    start = jnp.minimum((offset // 16) * 16, 2 * rows - span)
    local = pl.multiple_of(jnp.clip(start - (1 - mine) * rows, 0, rows - span), 16)
    there = pl.ds(pl.multiple_of((1 - mine) * rows + local, 16), span)
    factor = factor_ref[pl.ds(local, span), :1]
    project(h_ref, pl.ds(local, span), gain_ref, wk_ref, wv_ref, acc_k, acc_v, factor, chunk)
    keys, values = finish(cos_ref[there, :], sin_ref[there, :], acc_k, acc_v)
    kv[there, :cols] = keys
    kv[there, cols:] = values
    select_block(block, cols, owner, (offset_ref, length_ref, owner_ref, slot_ref), kv, block_ref)


def first_block(owner, block, places, peer, wk, wv, gain, cosine, sine, own, factor, chunk=1024):
    rows, width = peer.shape
    cols = wk.shape[1]
    span = block + 16
    return pl.pallas_call(
        functools.partial(first_kernel, owner, block, chunk),
        in_specs=[SMEM] * 4 + [VMEM] * 8,
        out_specs=VMEM,
        out_shape=jax.ShapeDtypeStruct((2, block, cols), jnp.bfloat16),
        scratch_shapes=[
            pltpu.VMEM((2 * rows, 2 * cols), jnp.bfloat16),
            pltpu.VMEM((span, cols), jnp.float32),
            pltpu.VMEM((span, cols), jnp.float32),
        ],
        compiler_params=pltpu.CompilerParams(vmem_limit_bytes=28 * MIB),
        cost_estimate=pl.CostEstimate(
            flops=4 * span * width * cols, bytes_accessed=2 * (span * width + 2 * width * cols), transcendentals=0
        ),
        name="first_block",
    )(*places, peer, wk, wv, gain, cosine, sine, own, factor)


def peer_kernel(
    far, block, chunk, offset_ref, length_ref, owner_ref, slot_ref,
    h_ref, wk_ref, wv_ref, gain_ref, cos_ref, sin_ref, own_ref, factor_ref, kv_ref, *rest
):
    blocks, (acc_k, acc_v) = rest[: len(far)], rest[len(far) :]
    rows, width = h_ref.shape
    cols = acc_k.shape[1]
    mine = lax.axis_index("tensor")
    there = pl.ds(pl.multiple_of((1 - mine) * rows, rows), rows)
    here = pl.ds(pl.multiple_of(mine * rows, rows), rows)
    project(h_ref, slice(None), gain_ref, wk_ref, wv_ref, acc_k, acc_v, factor_ref[:, :1], chunk)
    keys, values = finish(cos_ref[there, :], sin_ref[there, :], acc_k, acc_v)
    kv_ref[there, :cols] = keys
    kv_ref[there, cols:] = values
    kv_ref[here, :] = own_ref[...]
    places = (offset_ref, length_ref, owner_ref, slot_ref)
    for k, out_ref in zip(far, blocks):
        select_block(block, cols, jnp.bitwise_xor(lax.axis_index("dp"), k), places, kv_ref, out_ref)


def peer_rows(far, block, places, peer, wk, wv, gain, cosine, sine, own, factor, chunk=1024):
    rows, width = peer.shape
    cols = wk.shape[1]
    tok_rows = cosine.shape[0]
    return pl.pallas_call(
        functools.partial(peer_kernel, far, block, chunk),
        in_specs=[SMEM] * 4 + [VMEM] * 8,
        out_specs=[VMEM] * (1 + len(far)),
        out_shape=[jax.ShapeDtypeStruct((tok_rows, 2 * cols), jnp.bfloat16)]
        + [jax.ShapeDtypeStruct((2, block, cols), jnp.bfloat16)] * len(far),
        scratch_shapes=[
            pltpu.VMEM((rows, cols), jnp.float32),
            pltpu.VMEM((rows, cols), jnp.float32),
        ],
        compiler_params=pltpu.CompilerParams(vmem_limit_bytes=28 * MIB),
        cost_estimate=pl.CostEstimate(
            flops=4 * rows * width * cols, bytes_accessed=2 * (rows * width + 2 * width * cols), transcendentals=0
        ),
        name="peer_rows",
    )(*places, peer, wk, wv, gain, cosine, sine, own, factor)


def rest_kernel(owners, block, offset_ref, length_ref, owner_ref, slot_ref, kv_ref, *blocks):
    cols = kv_ref.shape[1] // 2
    places = (offset_ref, length_ref, owner_ref, slot_ref)
    for k, out_ref in zip(owners, blocks):
        select_block(block, cols, jnp.bitwise_xor(lax.axis_index("dp"), k), places, kv_ref, out_ref)


def rest_blocks(owners, block, places, kv):
    one = jax.ShapeDtypeStruct((2, block, kv.shape[1] // 2), jnp.bfloat16)
    return pl.pallas_call(
        functools.partial(rest_kernel, owners, block),
        in_specs=[SMEM] * 4 + [VMEM],
        out_specs=[VMEM] * len(owners),
        out_shape=[one] * len(owners),
        compiler_params=pltpu.CompilerParams(vmem_limit_bytes=28 * MIB),
        name="rest_blocks",
    )(*places, kv)


def attend_kernel(tile, window, offset_ref, q_ref, kv_ref, out_ref):
    cols = kv_ref.shape[1] // 2
    groups = cols // HD
    heads = q_ref.shape[1] // HD // groups
    first = pl.program_id(0) * tile
    start = pl.multiple_of(jnp.maximum(first + tile - window, 0), 16)
    row = first + lax.broadcasted_iota(jnp.int32, (tile, window), 0)
    key = start + lax.broadcasted_iota(jnp.int32, (tile, window), 1)
    allowed = (key <= row) & (key >= prompt_start(row, offset_ref))
    bias = jnp.where(allowed, 0.0, -1e30)[None]
    ones = jnp.ones((window, HD), jnp.bfloat16)
    scale = HD**-0.5 * float(np.log2(np.e))
    for g in range(groups):
        at = [slice((g * heads + h) * HD, (g * heads + h + 1) * HD) for h in range(heads)]
        q = jnp.concatenate([q_ref[:, a] for a in at], axis=0)
        k = kv_ref[pl.ds(start, window), g * HD : (g + 1) * HD]
        v = kv_ref[pl.ds(start, window), cols + g * HD : cols + (g + 1) * HD]
        scores = lax.dot_general(q, k, (((1,), (1,)), ((), ())), preferred_element_type=jnp.float32)
        scores = scores.reshape(heads, tile, window) * scale + bias
        exponent = jnp.exp2(scores - jnp.max(scores, axis=2, keepdims=True))
        exponent = exponent.astype(jnp.bfloat16).reshape(heads * tile, window)
        summed = jnp.dot(exponent, jnp.concatenate([v, ones], axis=1), preferred_element_type=jnp.float32)
        result = (summed[:, :HD] / summed[:, HD:]).astype(jnp.bfloat16)
        for h, a in enumerate(at):
            out_ref[:, a] = result[h * tile : (h + 1) * tile]


def attend(offsets, queries, kv, longest, tile=64):
    rows, width = queries.shape
    window = tile + longest
    rows_at = pl.BlockSpec((tile, width), lambda i: (i, 0))
    return pl.pallas_call(
        functools.partial(attend_kernel, tile, window),
        grid=(rows // tile,),
        in_specs=[SMEM, rows_at, pl.BlockSpec(kv.shape, lambda i: (0, 0))],
        out_specs=rows_at,
        out_shape=jax.ShapeDtypeStruct((rows, width), jnp.bfloat16),
        compiler_params=pltpu.CompilerParams(vmem_limit_bytes=32 * MIB),
        cost_estimate=pl.CostEstimate(
            flops=4 * rows * width * window,
            bytes_accessed=4 * rows * width,
            transcendentals=rows * window * width // HD,
        ),
        name="attend",
    )(offsets, queries, kv)


def gather_kernel(order, block, *refs):
    key_ref, value_ref, sems = refs[-3:]
    me = lax.axis_index("dp")
    copies = []
    for i, k in enumerate(order):
        rows = pl.ds(pl.multiple_of(jnp.bitwise_xor(me, k) * block, block), block)
        for n, out_ref in enumerate((key_ref, value_ref)):
            copies.append(pltpu.make_async_copy(refs[i].at[n], out_ref.at[rows, :], sems.at[i, n]))
    for copy in copies:
        copy.start()
    for copy in copies:
        copy.wait()


def place(order, block, blocks, cache, before=()):
    n = len(order)
    anywhere = pl.BlockSpec(memory_space=pl.ANY)
    return pl.pallas_call(
        functools.partial(gather_kernel, order, block),
        in_specs=[VMEM] * n + [anywhere] * len(before),
        out_specs=[anywhere] * 2,
        out_shape=[cache, cache],
        input_output_aliases={n: 0, n + 1: 1} if before else {},
        scratch_shapes=[pltpu.SemaphoreType.DMA((n, 2))],
        compiler_params=pltpu.CompilerParams(vmem_limit_bytes=8 * MIB),
        name="place_rest" if before else "place_first",
    )(*blocks, *before)


def on_device(
    hidden, norm_gain, key_weight, value_weight, queries,
    segment_ids, prompt_lengths, prompt_offsets, decode_owner, slot_offsets,
):
    n_dp = lax.axis_size("dp")
    half, width = hidden.shape
    tok_rows = queries.shape[0]
    cols = key_weight.shape[1]
    block = 2 * tok_rows // n_dp
    gain = norm_gain.reshape(1, width)

    peer = lax.ppermute(hidden, "tensor", [(0, 1), (1, 0)])
    own_k, own_v, factor, wk, wv = own_rows(hidden, key_weight, value_weight, gain)
    own, cosine, sine = rotate_own(block, prompt_offsets, own_k, own_v)
    places = [prompt_offsets, prompt_lengths, decode_owner, slot_offsets]
    swap = lambda a, k: lax.ppermute(a, "dp", [(p, p ^ k) for p in range(n_dp)]) if k else a
    half_dp = n_dp // 2
    far = list(range(half_dp, n_dp))
    near = list(range(1, half_dp))
    order = (far[2], far[1], *near[1:], far[0], *far[3:], near[0], 0)
    factor = lax.ppermute(factor, "tensor", [(0, 1), (1, 0)])
    first = first_block(order[0], block, places, peer, wk, wv, gain, cosine, sine, own, factor)
    kv, *blocks = peer_rows(order[1:5], block, places, peer, wk, wv, gain, cosine, sine, own, factor)
    first, later = lax.optimization_barrier((swap(first, order[0]), kv))
    blocks += rest_blocks(order[5:], block, places, later)
    received = [first] + [swap(a, k) for k, a in zip(order[1:], blocks)]
    attended = attend(prompt_offsets, queries, kv, block)
    cache = jax.ShapeDtypeStruct((n_dp * block, cols), jnp.bfloat16)
    by_place = dict(zip(order, received))
    early = (0, *order[: n_dp // 2 + 1])
    late = tuple(k for k in order if k not in early)
    caches = place(early, block, [by_place[k] for k in early], cache)
    key_cache, value_cache = place(late, block, [by_place[k] for k in late], cache, caches)
    return attended, key_cache[None], value_cache[None]


def solution(mesh):
    rows = P(("groups", "dp"))
    in_specs = (
        P(("groups", "dp", "tensor"), None),
        P(),
        P(None, "tensor"),
        P(None, "tensor"),
        P(("groups", "dp"), "tensor"),
        rows, rows, rows, rows, rows,
    )
    out_specs = (
        P(("groups", "dp"), "tensor"),
        P(("groups", "dp"), None, "tensor"),
        P(("groups", "dp"), None, "tensor"),
    )
    return jax.shard_map(on_device, mesh=mesh, in_specs=in_specs, out_specs=out_specs, check_vma=False)
```
